512 devices in a mesh: tm: 16 (over z, core), chan: 32 (over y, x).
Axes of the slice: x: 4, y: 8, z: 8, core: 2. Of those that a mesh axis runs over, the one named last changes fastest.
Arguments:
- raw: bfloat16 [65536, 8192], P('chan', 'tm'), may hold values from -6 to 6
- band_taps: float32 [3, 257], replicated, may hold values from -0.375 to 0.375
- band_gain: float32 [16], replicated, may hold values from 0.25 to 4
- gain_index: int32 [65536, 3], P('chan'), may hold values from 0 to 15
- owner_of: int32 [65536, 1], replicated, may hold values from 0 to 31; in each aligned block of 128 rows (0 to 127, 128 to 255, ...) at most 8 rows name the same one
- seat: int32 [65536], replicated, may hold values from 0 to 4
- cable_length: int32 [160], P('chan'), may hold values from 8 to 63
Outputs:
- cable_series: float32 [160, 8192], P('chan', 'tm')
The draws below stay inside these ranges and needn't reach their ends.
Inputs may be any that keep to these rules, and one draw needn't show every extreme that they name: `owner_of`: among the channels of one device (aligned blocks of 128 channel numbers c = (j * 16 + t) * 128 + i), at most 8 have one owner, and some owner has exactly 8; every owner is used.
All inputs are finite; a program needn't handle non-finite values.
Results may differ from the reference program's by a relative error of at most 0.0066.
Values may be sent and summed in bfloat16 or wider, within the bound.
No kernel may reach another device: no remote copies, remote signals or barrier semaphores. Data moves between devices by JAX's collectives and lax.ppermute only.
A program may use at most 128 MiB of HBM per device.

```python
import math
import jax
import jax.numpy as jnp
import numpy as np
from jax import lax

CH_DEV = 128
CAB_DEV = 5
TAPS = 257
BANDS = 3
LEVELS = 16
CHANNELS = 65536
SAMPLES = 8192
CABLES = 160
CAP = 8
N_TM = 16
N_CHAN = 32


def plant(array, rng, low, largest):
    spot = [jax.random.randint(jax.random.fold_in(rng, axis), (), 0, length) for axis, length in enumerate(array.shape)]
    longest = array.shape.index(max(array.shape))
    next_to = spot[:longest] + [(spot[longest] + 1) % array.shape[longest]] + spot[longest + 1:]
    return array.at[tuple(spot)].set(low).at[tuple(next_to)].set(largest)


def steps_of(rng, dims, pieces, least, top_value):
    def one(axis_at, shards_of):
        draws = jax.random.uniform(jax.random.fold_in(jax.random.fold_in(rng, 6), axis_at), (shards_of,), jnp.float32, least / len(pieces), top_value / len(pieces))
        return jnp.repeat(jnp.exp(draws), dims[axis_at] // shards_of).reshape((-1,) + (1,) * (len(dims) - axis_at - 1))

    factor_of = one(*pieces[0])
    for cut in pieces[1:]:
        factor_of = factor_of * one(*cut)
    return factor_of


def shared_out(stream_key, own, number, rows, count, top, reach, lean):
    ranking = jax.random.permutation(stream_key, count)
    heavy_load, common = load_shares(count, rows * top, reach, lean, True), load_shares(count, rows * top, reach, lean, False)
    places = jnp.arange(count)

    def named(lengths, offset_by):
        used = int((lengths > 0).sum())
        fixed = max(1, used // 4)
        passed = fixed + (places - fixed + offset_by * (used - fixed)) % max(1, count - fixed)
        return jnp.zeros((count,), jnp.int32).at[ranking[jnp.where(places < fixed, places, passed)]].set(jnp.asarray(lengths, jnp.int32))

    lengths = jnp.where(number % 4 == 0, named(heavy_load, number // 4), named(common, number - number // 4 - 1))
    mixed = jax.random.permutation(jax.random.fold_in(own, 3), count)
    source_of, receiver = mixed[0:count // 2 * 2:2], mixed[1:count // 2 * 2:2]
    slack = jnp.minimum(lengths[source_of] - 1, reach - lengths[receiver]) // 2
    slack = jnp.where((source_of == ranking[0]) | (receiver == ranking[0]) | (lengths[receiver] == 0), 0, jnp.maximum(slack, 0))
    passed = jax.random.randint(jax.random.fold_in(own, 4), (count // 2,), 0, 1 << 20) % (slack + 1)
    lengths = lengths.at[source_of].add(-passed).at[receiver].add(passed)
    members = jnp.searchsorted(jnp.cumsum(lengths), jnp.arange(rows * top), side="right").astype(jnp.int32)
    table = members.reshape(top, rows).T
    table = table[jax.random.permutation(jax.random.fold_in(own, 1), rows)]
    offset_by = jax.random.randint(jax.random.fold_in(own, 2), (rows, 1), 0, top)
    return jnp.take_along_axis(table, (jnp.arange(top)[None, :] + offset_by) % top, axis=1)


def load_shares(count, total, reach, skew, full):
    portions = [(1 << 20) // math.isqrt(grade ** skew) + 1 for grade in range(1, count + 1)]
    largest = reach if full else min(reach, max(-(-total // count), total * portions[0] // sum(portions)))
    least = 1 if total - largest >= count - 1 else 0
    counts, spare = [largest] + [least] * (count - 1), total - largest - least * (count - 1)
    while spare > 0:
        candidates = [i for i in range(1, count) if counts[i] < largest] or [i for i in range(1, count) if counts[i] < reach]
        mass, left = sum([portions[i] for i in candidates]), spare
        for i in candidates:
            addition = min(reach - counts[i], max(1, left * portions[i] // mass), spare)
            counts[i] = counts[i] + addition
            spare = spare - addition
    return np.array(counts)


def centred(key, shape, deviation, limit, split=(), kind=jnp.bfloat16):
    level = steps_of(key, shape, split, -0.22, 0.18) if split else 1.0
    result = jax.random.normal(key, shape, jnp.float32) * deviation * level
    return jnp.minimum(jnp.maximum(result, -limit), limit).astype(kind)


def setup_inputs(seed: int = 0) -> dict:
    arg_keys = jax.random.split(jax.random.key(seed), 8)
    raw = centred(arg_keys[0], (CHANNELS, SAMPLES), 1.0, 6.0, ((0, 32), (1, 16)))
    band_taps = centred(arg_keys[1], (BANDS, TAPS), TAPS ** -0.5, 0.375, (), jnp.float32)
    band_gain = jnp.clip(jnp.exp(jax.random.uniform(arg_keys[2], (LEVELS,), jnp.float32, math.log(0.25), math.log(4.0))), 0.25, 4.0)
    gain_index = plant(jax.random.randint(arg_keys[3], (CHANNELS, BANDS), 0, LEVELS), jax.random.fold_in(arg_keys[3], 1), 0, LEVELS - 1).astype(jnp.int32)
    owner_of_keys = jax.random.split(jax.random.fold_in(arg_keys[4], 1), CHANNELS // CH_DEV)
    owner_of_turns = jax.random.permutation(jax.random.fold_in(arg_keys[4], 3), CHANNELS // CH_DEV)
    owner_of = jax.vmap(lambda own, number: shared_out(jax.random.fold_in(arg_keys[4], 2), own, number, CH_DEV, N_CHAN, 1, CAP, 2))(owner_of_keys, owner_of_turns).reshape((CHANNELS, 1))
    seat = plant(jax.random.randint(arg_keys[5], (CHANNELS,), 0, CAB_DEV), jax.random.fold_in(arg_keys[5], 1), 0, CAB_DEV - 1).astype(jnp.int32)
    cable_length = plant(jax.random.randint(arg_keys[6], (CABLES,), 8, 64), jax.random.fold_in(arg_keys[6], 1), 8, 63).astype(jnp.int32)
    return {"raw": raw, "band_taps": band_taps, "band_gain": band_gain, "gain_index": gain_index, "owner_of": owner_of, "seat": seat, "cable_length": cable_length}


def reference(raw, band_taps, band_gain, gain_index, owner_of, seat, cable_length):
    tap_values = lax.optimization_barrier(band_taps.astype(jnp.bfloat16)).astype(jnp.float32)
    half_width = TAPS // 2
    samples = raw.shape[1]
    fft_length = samples + TAPS - 1
    spectrum = jnp.fft.rfft(tap_values, n=fft_length, axis=1)
    gain_rows = band_gain[gain_index]
    cable = (owner_of[:, 0] * CAB_DEV + seat).astype(jnp.int32)
    block_len = CH_DEV * N_TM
    block_count = CHANNELS // block_len

    def accumulate(running, block_index):
        first_row = (block_index * block_len).astype(jnp.int32)
        signal = lax.dynamic_slice_in_dim(raw, first_row, block_len, 0).astype(jnp.float32)
        gains_blk = lax.dynamic_slice_in_dim(gain_rows, first_row, block_len, 0)
        cable_blk = lax.dynamic_slice_in_dim(cable, first_row, block_len, 0)
        signal_spec = jnp.fft.rfft(signal, n=fft_length, axis=1)
        convolved = jnp.fft.irfft(signal_spec[:, None, :] * spectrum[None], n=fft_length, axis=2)
        convolved = convolved[:, :, half_width:half_width + samples]
        filtered = gains_blk[:, 0:1] * convolved[:, 0] + gains_blk[:, 1:2] * convolved[:, 1] + gains_blk[:, 2:3] * convolved[:, 2]
        padded_edges = jnp.pad(filtered, ((0, 0), (1, 1)))
        strain_rate = (0.5 * (padded_edges[:, 2:] - padded_edges[:, :-2])).astype(jnp.bfloat16)
        rate_values = strain_rate.astype(jnp.float32)
        power = rate_values * jnp.abs(rate_values)
        running = running + jax.ops.segment_sum(power, cable_blk, num_segments=CABLES)
        return running, None

    start_sum = jnp.zeros((CABLES, samples), jnp.float32)
    cable_sum, unused = lax.scan(accumulate, start_sum, jnp.arange(block_count, dtype=jnp.int32))
    return cable_sum / cable_length.astype(jnp.float32)[:, None]
```

```python
import functools

import jax
import jax.numpy as jnp
from jax import lax
from jax.experimental import pallas as pl
from jax.experimental.pallas import tpu as pltpu
from jax.sharding import PartitionSpec as P

LANES = 128
SIDE = 144
INNER = 256
SIDE_COLS = 2048
INNER_COLS = 2048
F32 = jnp.float32
BF16 = jnp.bfloat16
NT = (((1,), (1,)), ((), ()))


def beside_rows(beside, lane_at):
    count = beside.shape[0]
    lane = lax.broadcasted_iota(jnp.int32, (16, LANES), 1)
    pick = (lane == lane_at).astype(F32).astype(BF16)
    column = lax.dot_general(pick, beside, NT, preferred_element_type=F32)
    rows = [column[0:1, a * LANES : (a + 1) * LANES] for a in range(count // LANES)]
    return jnp.concatenate(rows, axis=0).astype(BF16)


def is_low_core():
    return lax.axis_index("tm") % 2 == 0


def pack_kernel(is_far, raw_ref, *refs):
    strip_ref = refs[-1]
    count = raw_ref.shape[0]
    core = lax.axis_index("tm") % 2
    side = core if is_far else 1 - core
    strip_ref[0:count, :] = raw_ref[:, pl.ds(pl.multiple_of(side * (3 * LANES), LANES), LANES)]
    beside = raw_ref[:, pl.ds(pl.multiple_of(LANES + side * LANES, LANES), LANES)]
    strip_ref[count:, :] = beside_rows(beside, side * (LANES - 1))


def pack(raw, is_far, *after):
    count, depth = raw.shape
    vmem = pl.BlockSpec(memory_space=pltpu.VMEM)
    return pl.pallas_call(
        functools.partial(pack_kernel, is_far),
        in_specs=[vmem] + [pl.BlockSpec(memory_space=pl.ANY)] * len(after),
        out_specs=vmem,
        out_shape=jax.ShapeDtypeStruct((count + 16, LANES), BF16),
        compiler_params=pltpu.CompilerParams(vmem_limit_bytes=8 << 20),
        cost_estimate=pl.CostEstimate(
            flops=2 * count * depth * 768, bytes_accessed=4 << 20, transcendentals=0
        ),
        name="far_strip" if is_far else "near_strip",
    )(raw, *after)


def window_sums(columns_of, taps_ref, size, gains_ref, edges_of, onehot_ref, count, step):
    sub = lax.broadcasted_iota(jnp.int32, (8, step), 0)
    total = None
    for start in range(0, count, step):
        part = slice(start, start + step)
        bands = lax.dot_general(taps_ref[...], columns_of(part), NT, preferred_element_type=F32)
        held = gains_ref[0:1, part] * bands[0:size]
        for b in (1, 2):
            held = held + gains_ref[b : b + 1, part] * bands[b * size : (b + 1) * size]
        first, last = held[0:8], held[size - 8 : size]
        if edges_of is not None:
            low, high = edges_of(start)
            first = first + jnp.where(sub == 0, low, 0.0)
            last = last + jnp.where(sub == 7, high, 0.0)
        middle = held[8 : size - 8]
        ahead = jnp.concatenate([middle, last, pltpu.roll(first, 7, 0)], axis=0)
        behind = jnp.concatenate([pltpu.roll(last, 1, 0), first, middle], axis=0)
        rate = (ahead - behind).astype(BF16)
        power = rate * jnp.abs(rate)
        term = lax.dot_general(onehot_ref[:, part], power, NT, preferred_element_type=F32)
        total = term if total is None else total + term
    return total


def sample_of_row(rows, size, cols):
    row = lax.broadcasted_iota(jnp.int32, (rows, cols), 0)
    return jnp.bitwise_and(row, 7) * (size // 8) + jnp.right_shift(row, 3)


def prepare_kernel(
    levels_ref, taps_ref, index_ref, place_ref,
    inner_taps_ref, far_taps_ref, near_taps_ref, gains_ref, onehot_ref,
):
    is_low = is_low_core()
    tm_pos = lax.axis_index("tm")
    inside = jnp.logical_and(tm_pos > 0, tm_pos < lax.axis_size("tm") - 1).astype(F32)
    count = index_ref.shape[1]
    depth = inner_taps_ref.shape[1]
    bands, width = taps_ref.shape
    blocks = count // LANES
    wide = depth + LANES

    reach = 3 * LANES
    lane = lax.broadcasted_iota(jnp.int32, (bands, reach - 2 * LANES), 1)
    tail = jnp.where(lane == 0, taps_ref[:, width - 1 : width], 0.0)
    taps = jnp.concatenate([taps_ref[:, 0 : width - 1], tail], axis=1).astype(BF16)
    turn = (
        lax.broadcasted_iota(jnp.int32, (reach, wide), 0) + lax.broadcasted_iota(jnp.int32, (reach, wide), 1)
        == width - 1
    )
    base = jnp.dot(taps, turn.astype(F32).astype(BF16), preferred_element_type=F32)
    sub = lax.broadcasted_iota(jnp.int32, (8, depth), 0)

    row = lax.broadcasted_iota(jnp.int32, (8, wide), 0)

    def rows_of(b, size, shifts):
        line = jnp.broadcast_to(base[b : b + 1, :], (8, wide))
        spread = size // 8
        fan = line
        for i in range(1, 8):
            fan = jnp.where(row == i, pltpu.roll(line, i * spread, 1), fan)
        return [
            [pltpu.roll(fan, (j + shift) % wide, 1)[:, 0:depth] for j in range(spread)]
            for shift in shifts
        ]

    for b in range(bands):
        (rows,) = rows_of(b, INNER, (0,))
        for j in range(0, INNER // 8, 2):
            at = b * INNER + 8 * j
            inner_taps_ref[at : at + 16, :] = jnp.concatenate(rows[j : j + 2], axis=0).astype(BF16)
        low, high = rows_of(b, SIDE, (-1, 2 * LANES + 1 - SIDE))
        low[0] = jnp.where(sub == 0, low[0] * jnp.where(is_low, inside, 1.0), low[0])
        high[-1] = jnp.where(sub == 7, high[-1] * jnp.where(is_low, 1.0, inside), high[-1])
        for j in range(0, SIDE // 8, 2):
            at = slice(b * SIDE + 8 * j, b * SIDE + 8 * j + 16)
            low_rows = jnp.concatenate(low[j : j + 2], axis=0).astype(BF16)
            high_rows = jnp.concatenate(high[j : j + 2], axis=0).astype(BF16)
            high_rows = jnp.concatenate([high_rows[:, 3 * LANES :], high_rows[:, : 3 * LANES]], axis=1)

            @pl.when(is_low)
            def _():
                far_taps_ref[at, :] = low_rows
                near_taps_ref[at, :] = high_rows

            @pl.when(jnp.logical_not(is_low))
            def _():
                far_taps_ref[at, :] = high_rows
                near_taps_ref[at, :] = low_rows

    index = index_ref[...]
    gains = jnp.zeros(index.shape, F32)
    for level in range(levels_ref.shape[0]):
        gains = jnp.where(index == level, levels_ref[level], gains)
    gains = 0.5 * gains
    first = taps_ref[:, 0:1].astype(BF16).astype(F32)
    final = taps_ref[:, width - 1 : width].astype(BF16).astype(F32)
    low_edge = jnp.sum(gains * final, axis=0, keepdims=True)
    high_edge = jnp.sum(gains * first, axis=0, keepdims=True)
    gains_ref[0:bands, :] = gains
    gains_ref[3:4, :] = jnp.where(is_low, low_edge, high_edge)
    gains_ref[4:5, :] = jnp.where(is_low, high_edge, low_edge)
    place = place_ref[...]
    cable = lax.broadcasted_iota(jnp.int32, (onehot_ref.shape[0], LANES), 0)
    for a in range(blocks):
        onehot_ref[:, a * LANES : (a + 1) * LANES] = (cable == place[a : a + 1, :]).astype(F32).astype(BF16)


def prepare(band_gain, taps, index, place, cables, depth):
    count = index.shape[1]
    bands = taps.shape[0]
    smem = pl.BlockSpec(memory_space=pltpu.SMEM)
    vmem = pl.BlockSpec(memory_space=pltpu.VMEM)
    outs = [
        ((bands * INNER, depth), BF16),
        ((bands * SIDE, depth), BF16),
        ((bands * SIDE, depth), BF16),
        ((8, count), F32),
        ((cables, count), BF16),
    ]
    return pl.pallas_call(
        prepare_kernel,
        in_specs=[smem] + [vmem] * 3,
        out_specs=[vmem] * len(outs),
        out_shape=[jax.ShapeDtypeStruct(s, d) for s, d in outs],
        compiler_params=pltpu.CompilerParams(vmem_limit_bytes=16 << 20),
        cost_estimate=pl.CostEstimate(
            flops=2 * count * depth * bands * INNER, bytes_accessed=6 << 20, transcendentals=0
        ),
        name="prepare",
    )(band_gain, taps, index, place)


def inner_kernel(raw_ref, taps_ref, gains_ref, onehot_ref, sums_ref):
    count = raw_ref.shape[0]
    sums_ref[...] = window_sums(
        lambda part: raw_ref[part, :], taps_ref, INNER, gains_ref, None, onehot_ref, count, INNER_COLS
    )


def side_sums(is_low, edge_row, raw_ref, strip_ref, taps_ref, gains_ref, onehot_ref):
    count = raw_ref.shape[0]
    offset = pl.multiple_of(jnp.where(is_low, 0, LANES), LANES)
    beside = strip_ref[count:, :].astype(F32)

    def columns_of(part):
        return jnp.concatenate([strip_ref[part, :], raw_ref[part, pl.ds(offset, 3 * LANES)]], axis=1)

    def edges_of(start):
        rows = range(start // LANES, (start + SIDE_COLS) // LANES)
        line = jnp.concatenate([beside[a : a + 1, :] for a in rows], axis=1)
        line = line * gains_ref[edge_row : edge_row + 1, start : start + SIDE_COLS]
        return jnp.where(is_low, line, 0.0), jnp.where(is_low, 0.0, line)

    sums = window_sums(
        columns_of, taps_ref, SIDE, gains_ref, edges_of, onehot_ref, count, SIDE_COLS
    )
    depth = raw_ref.shape[1]
    sample = sample_of_row(SIDE, SIDE, depth)
    sample = sample + jnp.where(is_low, -1, depth + 1 - SIDE)
    kept = (sample >= jnp.where(is_low, 0, depth - 1 - LANES)) & (
        sample <= jnp.where(is_low, LANES, depth - 1)
    )
    col = lax.broadcasted_iota(jnp.int32, (SIDE, depth), 1)
    order = ((col == sample) & kept).astype(F32).astype(BF16)
    return jnp.dot(sums.astype(BF16), order, preferred_element_type=F32)


def near_kernel(raw_ref, strip_ref, taps_ref, gains_ref, onehot_ref, inner_ref, sums_ref):
    near = side_sums(jnp.logical_not(is_low_core()), 4, raw_ref, strip_ref, taps_ref, gains_ref, onehot_ref)
    depth = raw_ref.shape[1]
    sample = sample_of_row(INNER, INNER, depth) + LANES
    kept = (sample > LANES) & (sample < depth - LANES - 1)
    col = lax.broadcasted_iota(jnp.int32, (INNER, depth), 1)
    order = ((col == sample) & kept).astype(F32).astype(BF16)
    sums_ref[...] = near + jnp.dot(inner_ref[...].astype(BF16), order, preferred_element_type=F32)


def far_kernel(
    raw_ref, strip_ref, taps_ref, gains_ref, onehot_ref, others_ref, out_ref, scr
):
    owners, pitch, _ = out_ref.shape
    seats = others_ref.shape[0] // owners
    far = side_sums(is_low_core(), 3, raw_ref, strip_ref, taps_ref, gains_ref, onehot_ref)
    sums = others_ref[...] + far
    scr[...] = jnp.zeros_like(scr)
    tiles = sums.shape[1] // LANES
    for s in range(seats):
        for j in range(tiles):
            scr[pl.ds(tiles * s + j, owners, stride=pitch), :] = sums[
                s * owners : (s + 1) * owners, j * LANES : (j + 1) * LANES
            ]
    for o in range(owners):
        out_ref[o, :, :] = scr[o * pitch : (o + 1) * pitch, :].astype(BF16)


def window(kernel, name, out_shape, scratch, taps_at, args):
    count, depth = args[0].shape
    vmem = pl.BlockSpec(memory_space=pltpu.VMEM)
    return pl.pallas_call(
        kernel,
        in_specs=[vmem] * len(args),
        out_specs=vmem,
        out_shape=out_shape,
        scratch_shapes=scratch,
        compiler_params=pltpu.CompilerParams(vmem_limit_bytes=24 << 20),
        cost_estimate=pl.CostEstimate(
            flops=(50 if name == 'inner_window' else 1) * 2 * count * depth * 768, bytes_accessed=4<<20, transcendentals=0
        ),
        name=name,
    )(*args)


def finish_kernel(length_ref, parts_ref, out_ref):
    seats, depth = out_ref.shape
    tiles = depth // LANES
    total = jnp.sum(parts_ref[...].astype(F32), axis=0)
    for s in range(seats):
        length = length_ref[s].astype(F32)
        for j in range(tiles):
            row = tiles * s + j
            out_ref[s : s + 1, j * LANES : (j + 1) * LANES] = total[row : row + 1] / length


def finish(parts, cable_length, depth):
    return pl.pallas_call(
        finish_kernel,
        in_specs=[pl.BlockSpec(memory_space=pltpu.SMEM), pl.BlockSpec(memory_space=pltpu.VMEM)],
        out_specs=pl.BlockSpec(memory_space=pltpu.VMEM),
        out_shape=jax.ShapeDtypeStruct((cable_length.shape[0], depth), F32),
        compiler_params=pltpu.CompilerParams(vmem_limit_bytes=4 << 20),
        name="finish_sum",
    )(cable_length, parts)


def shards(raw, band_taps, band_gain, gain_index, owner_of, seat, cable_length):
    tm_count = lax.axis_size("tm")
    chan_count = lax.axis_size("chan")
    depth = raw.shape[1]
    far_pairs = [(i, i + 1) for i in range(1, tm_count - 1, 2)]
    far_pairs = far_pairs + [(j, i) for i, j in far_pairs]
    near_pairs = [(i, i ^ 1) for i in range(tm_count)]
    cab_dev = cable_length.shape[0]
    cables = cab_dev * chan_count

    blocks = raw.shape[0] // LANES
    mine = lax.axis_index("chan") * blocks
    place = lax.dynamic_slice_in_dim(seat.reshape(-1, LANES), mine, blocks, 0) * chan_count
    place = place + lax.dynamic_slice_in_dim(owner_of.reshape(-1, LANES), mine, blocks, 0)
    far_sent = pack(raw, True)
    far_strip = lax.ppermute(far_sent, "tm", far_pairs)
    near_strip = lax.ppermute(pack(raw, False, far_sent), "tm", near_pairs)
    inner_taps, far_taps, near_taps, gains, onehot = prepare(
        band_gain, band_taps, gain_index.T, place, cables, depth
    )
    inner_sums = window(
        inner_kernel, "inner_window", jax.ShapeDtypeStruct((cables, INNER), F32), [], 1,
        (raw, inner_taps, gains, onehot),
    )
    others = window(
        near_kernel, "near_window", jax.ShapeDtypeStruct((cables, depth), F32), [], 2,
        (raw, near_strip, near_taps, gains, onehot, inner_sums),
    )
    pitch = -(-(depth // LANES) * cab_dev // 8) * 8
    parts = window(
        far_kernel, "far_window", jax.ShapeDtypeStruct((chan_count, pitch, LANES), BF16),
        [pltpu.VMEM((chan_count * pitch, LANES), F32)], 2,
        (raw, far_strip, far_taps, gains, onehot, others),
    )
    parts = lax.all_to_all(parts, "chan", split_axis=0, concat_axis=0, tiled=True)
    return finish(parts, cable_length, depth)


def solution(mesh):
    return jax.shard_map(
        shards,
        mesh=mesh,
        in_specs=(P("chan", "tm"), P(), P(), P("chan", None), P(), P(), P("chan")),
        out_specs=P("chan", "tm"),
        check_vma=False,
    )
```

```python
import jax
import jax.numpy as jnp
from jax import lax
from jax.experimental import pallas as pl
from jax.experimental.pallas import tpu as pltpu
from jax.sharding import PartitionSpec as P

LANES = 128
SIDE = 144
INNER = 256
SIDE_COLS = 2048
INNER_COLS = 2048
F32 = jnp.float32
BF16 = jnp.bfloat16
NT = (((1,), (1,)), ((), ()))


def beside_rows(beside, lane_at):
    count = beside.shape[0]
    lane = lax.broadcasted_iota(jnp.int32, (16, LANES), 1)
    pick = (lane == lane_at).astype(F32).astype(BF16)
    column = lax.dot_general(pick, beside, NT, preferred_element_type=F32)
    rows = [column[0:1, a * LANES : (a + 1) * LANES] for a in range(count // LANES)]
    return jnp.concatenate(rows, axis=0).astype(BF16)


def is_low_core():
    return lax.axis_index("tm") % 2 == 0


def fill_strip(side, raw_ref, strip_ref):
    count = raw_ref.shape[0]
    strip_ref[0:count, :] = raw_ref[:, pl.ds(pl.multiple_of(side * (3 * LANES), LANES), LANES)]
    beside = raw_ref[:, pl.ds(pl.multiple_of(LANES + side * LANES, LANES), LANES)]
    strip_ref[count:, :] = beside_rows(beside, side * (LANES - 1))


def far_pack_kernel(raw_ref, token_ref, strip_ref):
    del token_ref
    fill_strip(lax.axis_index("tm") % 2, raw_ref, strip_ref)


def near_pack_kernel(
    raw_ref, after_ref, taps_ref, early_inner_ref, early_far_ref, early_near_ref,
    strip_ref, inner_taps_ref, far_taps_ref, near_taps_ref,
):
    del after_ref
    fill_strip(1 - lax.axis_index("tm") % 2, raw_ref, strip_ref)

    @pl.when(is_low_core())
    def _():
        build_taps(True, taps_ref, inner_taps_ref, far_taps_ref, near_taps_ref)

    @pl.when(jnp.logical_not(is_low_core()))
    def _():
        inner_taps_ref[...] = early_inner_ref[...]
        far_taps_ref[...] = early_far_ref[...]
        near_taps_ref[...] = early_near_ref[...]


def far_pack(raw, token):
    count = raw.shape[0]
    vmem = pl.BlockSpec(memory_space=pltpu.VMEM)
    return pl.pallas_call(
        far_pack_kernel,
        in_specs=[vmem, pl.BlockSpec(memory_space=pl.ANY)],
        out_specs=vmem,
        out_shape=jax.ShapeDtypeStruct((count + 16, LANES), BF16),
        compiler_params=pltpu.CompilerParams(vmem_limit_bytes=8 << 20),
        name="far_strip",
    )(raw, token)


def near_pack(raw, after, taps, early):
    count, depth = raw.shape
    vmem = pl.BlockSpec(memory_space=pltpu.VMEM)
    return pl.pallas_call(
        near_pack_kernel,
        in_specs=[vmem, pl.BlockSpec(memory_space=pl.ANY)] + [vmem] * 4,
        out_specs=[vmem] * 4,
        out_shape=[jax.ShapeDtypeStruct((count + 16, LANES), BF16)] + tap_shapes(taps, depth),
        compiler_params=pltpu.CompilerParams(vmem_limit_bytes=8 << 20),
        cost_estimate=pl.CostEstimate(
            flops=2 * count * depth * 768, bytes_accessed=4 << 20, transcendentals=0
        ),
        name="near_strip",
    )(raw, after, taps, *early)


def window_sums(columns_of, taps_ref, size, gains_ref, edges_of, onehot_ref, count, step):
    sub = lax.broadcasted_iota(jnp.int32, (8, step), 0)
    total = None
    for start in range(0, count, step):
        part = slice(start, start + step)
        bands = lax.dot_general(taps_ref[...], columns_of(part), NT, preferred_element_type=F32)
        held = gains_ref[0:1, part] * bands[0:size]
        for b in (1, 2):
            held = held + gains_ref[b : b + 1, part] * bands[b * size : (b + 1) * size]
        first, last = held[0:8], held[size - 8 : size]
        if edges_of is not None:
            low, high = edges_of(start)
            first = first + jnp.where(sub == 0, low, 0.0)
            last = last + jnp.where(sub == 7, high, 0.0)
        middle = held[8 : size - 8]
        ahead = jnp.concatenate([middle, last, pltpu.roll(first, 7, 0)], axis=0)
        behind = jnp.concatenate([pltpu.roll(last, 1, 0), first, middle], axis=0)
        rate = (ahead - behind).astype(BF16)
        power = rate * jnp.abs(rate)
        term = lax.dot_general(onehot_ref[:, part], power, NT, preferred_element_type=F32)
        total = term if total is None else total + term
    return total


def sample_of_row(rows, size, cols):
    row = lax.broadcasted_iota(jnp.int32, (rows, cols), 0)
    return jnp.bitwise_and(row, 7) * (size // 8) + jnp.right_shift(row, 3)


def build_taps(is_low, taps_ref, inner_taps_ref, far_taps_ref, near_taps_ref):
    tm_pos = lax.axis_index("tm")
    inside = jnp.logical_and(tm_pos > 0, tm_pos < lax.axis_size("tm") - 1).astype(F32)
    depth = inner_taps_ref.shape[1]
    bands, width = taps_ref.shape
    wide = depth + LANES

    reach = 3 * LANES
    lane = lax.broadcasted_iota(jnp.int32, (bands, reach - 2 * LANES), 1)
    tail = jnp.where(lane == 0, taps_ref[:, width - 1 : width], 0.0)
    taps = jnp.concatenate([taps_ref[:, 0 : width - 1], tail], axis=1).astype(BF16)
    turn = (
        lax.broadcasted_iota(jnp.int32, (reach, wide), 0) + lax.broadcasted_iota(jnp.int32, (reach, wide), 1)
        == width - 1
    )
    base = jnp.dot(taps, turn.astype(F32).astype(BF16), preferred_element_type=F32)
    sub = lax.broadcasted_iota(jnp.int32, (8, depth), 0)

    row = lax.broadcasted_iota(jnp.int32, (8, wide), 0)

    def rows_of(b, size, shifts):
        line = jnp.broadcast_to(base[b : b + 1, :], (8, wide))
        spread = size // 8
        fan = line
        for i in range(1, 8):
            fan = jnp.where(row == i, pltpu.roll(line, i * spread, 1), fan)
        return [
            [pltpu.roll(fan, (j + shift) % wide, 1)[:, 0:depth] for j in range(spread)]
            for shift in shifts
        ]

    for b in range(bands):
        (rows,) = rows_of(b, INNER, (0,))
        for j in range(0, INNER // 8, 2):
            at = b * INNER + 8 * j
            inner_taps_ref[at : at + 16, :] = jnp.concatenate(rows[j : j + 2], axis=0).astype(BF16)
        low, high = rows_of(b, SIDE, (-1, 2 * LANES + 1 - SIDE))
        if is_low:
            low[0] = jnp.where(sub == 0, low[0] * inside, low[0])
        else:
            high[-1] = jnp.where(sub == 7, high[-1] * inside, high[-1])
        for j in range(0, SIDE // 8, 2):
            at = slice(b * SIDE + 8 * j, b * SIDE + 8 * j + 16)
            low_rows = jnp.concatenate(low[j : j + 2], axis=0).astype(BF16)
            high_rows = jnp.concatenate(high[j : j + 2], axis=0).astype(BF16)
            high_rows = jnp.concatenate([high_rows[:, 3 * LANES :], high_rows[:, : 3 * LANES]], axis=1)

            far_taps_ref[at, :], near_taps_ref[at, :] = (
                (low_rows, high_rows) if is_low else (high_rows, low_rows)
            )


def early_taps_kernel(taps_ref, inner_taps_ref, far_taps_ref, near_taps_ref, token_ref):
    token_ref[...] = jnp.zeros_like(token_ref)

    @pl.when(jnp.logical_not(is_low_core()))
    def _():
        build_taps(False, taps_ref, inner_taps_ref, far_taps_ref, near_taps_ref)


def tap_shapes(taps, depth):
    rows = (INNER, SIDE, SIDE)
    return [jax.ShapeDtypeStruct((taps.shape[0] * r, depth), BF16) for r in rows]


def early_taps(taps, depth):
    vmem = pl.BlockSpec(memory_space=pltpu.VMEM)
    return pl.pallas_call(
        early_taps_kernel,
        in_specs=[vmem],
        out_specs=[vmem] * 4,
        out_shape=tap_shapes(taps, depth) + [jax.ShapeDtypeStruct((8, LANES), F32)],
        compiler_params=pltpu.CompilerParams(vmem_limit_bytes=8 << 20),
        cost_estimate=pl.CostEstimate(flops=3 << 30, bytes_accessed=6 << 20, transcendentals=0),
        name="early_taps",
    )(taps)


def channels_kernel(levels_ref, taps_ref, index_ref, owner_ref, seat_ref, gains_ref, onehot_ref):
    is_low = is_low_core()
    bands, width = taps_ref.shape
    blocks = index_ref.shape[1] // LANES
    index = index_ref[...]
    gains = jnp.zeros(index.shape, F32)
    for level in range(levels_ref.shape[0]):
        gains = jnp.where(index == level, levels_ref[level], gains)
    gains = 0.5 * gains
    first = taps_ref[:, 0:1].astype(BF16).astype(F32)
    final = taps_ref[:, width - 1 : width].astype(BF16).astype(F32)
    low_edge = jnp.sum(gains * final, axis=0, keepdims=True)
    high_edge = jnp.sum(gains * first, axis=0, keepdims=True)
    gains_ref[0:bands, :] = gains
    gains_ref[3:4, :] = jnp.where(is_low, low_edge, high_edge)
    gains_ref[4:5, :] = jnp.where(is_low, high_edge, low_edge)
    mine = pl.ds(pl.multiple_of(lax.axis_index("chan") * blocks, blocks), blocks)
    place = seat_ref[mine, :] * lax.axis_size("chan") + owner_ref[mine, :]
    cable = lax.broadcasted_iota(jnp.int32, (onehot_ref.shape[0], LANES), 0)
    for a in range(blocks):
        onehot_ref[:, a * LANES : (a + 1) * LANES] = (cable == place[a : a + 1, :]).astype(F32).astype(BF16)


def channel_tables(band_gain, taps, index, owner, seat, cables):
    count = index.shape[1]
    vmem = pl.BlockSpec(memory_space=pltpu.VMEM)
    return pl.pallas_call(
        channels_kernel,
        in_specs=[pl.BlockSpec(memory_space=pltpu.SMEM)] + [vmem] * 4,
        out_specs=[vmem] * 2,
        out_shape=[
            jax.ShapeDtypeStruct((8, count), F32),
            jax.ShapeDtypeStruct((cables, count), BF16),
        ],
        compiler_params=pltpu.CompilerParams(vmem_limit_bytes=8 << 20),
        cost_estimate=pl.CostEstimate(flops=1 << 30, bytes_accessed=1 << 20, transcendentals=0),
        name="channel_tables",
    )(band_gain, taps, index, owner, seat)


def inner_kernel(raw_ref, taps_ref, gains_ref, onehot_ref, sums_ref):
    count = raw_ref.shape[0]
    sums_ref[...] = window_sums(
        lambda part: raw_ref[part, :], taps_ref, INNER, gains_ref, None, onehot_ref, count, INNER_COLS
    )


def side_sums(is_low, edge_row, raw_ref, strip_ref, taps_ref, gains_ref, onehot_ref):
    count = raw_ref.shape[0]
    offset = pl.multiple_of(jnp.where(is_low, 0, LANES), LANES)
    beside = strip_ref[count:, :].astype(F32)

    def columns_of(part):
        return jnp.concatenate([strip_ref[part, :], raw_ref[part, pl.ds(offset, 3 * LANES)]], axis=1)

    def edges_of(start):
        rows = range(start // LANES, (start + SIDE_COLS) // LANES)
        line = jnp.concatenate([beside[a : a + 1, :] for a in rows], axis=1)
        line = line * gains_ref[edge_row : edge_row + 1, start : start + SIDE_COLS]
        return jnp.where(is_low, line, 0.0), jnp.where(is_low, 0.0, line)

    sums = window_sums(
        columns_of, taps_ref, SIDE, gains_ref, edges_of, onehot_ref, count, SIDE_COLS
    )
    depth = raw_ref.shape[1]
    sample = sample_of_row(SIDE, SIDE, depth)
    sample = sample + jnp.where(is_low, -1, depth + 1 - SIDE)
    kept = (sample >= jnp.where(is_low, 0, depth - 1 - LANES)) & (
        sample <= jnp.where(is_low, LANES, depth - 1)
    )
    col = lax.broadcasted_iota(jnp.int32, (SIDE, depth), 1)
    order = ((col == sample) & kept).astype(F32).astype(BF16)
    return jnp.dot(sums.astype(BF16), order, preferred_element_type=F32)


def near_kernel(raw_ref, strip_ref, taps_ref, gains_ref, onehot_ref, inner_ref, sums_ref):
    near = side_sums(jnp.logical_not(is_low_core()), 4, raw_ref, strip_ref, taps_ref, gains_ref, onehot_ref)
    depth = raw_ref.shape[1]
    sample = sample_of_row(INNER, INNER, depth) + LANES
    kept = (sample > LANES) & (sample < depth - LANES - 1)
    col = lax.broadcasted_iota(jnp.int32, (INNER, depth), 1)
    order = ((col == sample) & kept).astype(F32).astype(BF16)
    sums_ref[...] = near + jnp.dot(inner_ref[...].astype(BF16), order, preferred_element_type=F32)


def far_kernel(
    raw_ref, strip_ref, taps_ref, gains_ref, onehot_ref, others_ref, out_ref, scr
):
    owners, pitch, _ = out_ref.shape
    seats = others_ref.shape[0] // owners
    far = side_sums(is_low_core(), 3, raw_ref, strip_ref, taps_ref, gains_ref, onehot_ref)
    sums = others_ref[...] + far
    scr[...] = jnp.zeros_like(scr)
    tiles = sums.shape[1] // LANES
    for s in range(seats):
        for j in range(tiles):
            scr[pl.ds(tiles * s + j, owners, stride=pitch), :] = sums[
                s * owners : (s + 1) * owners, j * LANES : (j + 1) * LANES
            ]
    for o in range(owners):
        out_ref[o, :, :] = scr[o * pitch : (o + 1) * pitch, :].astype(BF16)


def window(kernel, name, out_shape, scratch, taps_at, args):
    count, depth = args[0].shape
    vmem = pl.BlockSpec(memory_space=pltpu.VMEM)
    return pl.pallas_call(
        kernel,
        in_specs=[vmem] * len(args),
        out_specs=vmem,
        out_shape=out_shape,
        scratch_shapes=scratch,
        compiler_params=pltpu.CompilerParams(vmem_limit_bytes=24 << 20),
        cost_estimate=pl.CostEstimate(
            flops=(50 if name == 'inner_window' else 1) * 2 * count * depth * 768, bytes_accessed=4<<20, transcendentals=0
        ),
        name=name,
    )(*args)


def finish_kernel(length_ref, parts_ref, out_ref):
    seats, depth = out_ref.shape
    tiles = depth // LANES
    total = jnp.sum(parts_ref[...].astype(F32), axis=0)
    for s in range(seats):
        length = length_ref[s].astype(F32)
        for j in range(tiles):
            row = tiles * s + j
            out_ref[s : s + 1, j * LANES : (j + 1) * LANES] = total[row : row + 1] / length


def finish(parts, cable_length, depth):
    return pl.pallas_call(
        finish_kernel,
        in_specs=[pl.BlockSpec(memory_space=pltpu.SMEM), pl.BlockSpec(memory_space=pltpu.VMEM)],
        out_specs=pl.BlockSpec(memory_space=pltpu.VMEM),
        out_shape=jax.ShapeDtypeStruct((cable_length.shape[0], depth), F32),
        compiler_params=pltpu.CompilerParams(vmem_limit_bytes=4 << 20),
        name="finish_sum",
    )(cable_length, parts)


def shards(raw, band_taps, band_gain, gain_index, owner_of, seat, cable_length):
    tm_count = lax.axis_size("tm")
    chan_count = lax.axis_size("chan")
    depth = raw.shape[1]
    far_pairs = [(i, i + 1) for i in range(1, tm_count - 1, 2)]
    far_pairs = far_pairs + [(j, i) for i, j in far_pairs]
    near_pairs = [(i, i ^ 1) for i in range(tm_count)]
    cab_dev = cable_length.shape[0]
    cables = cab_dev * chan_count

    *early, token = early_taps(band_taps, depth)
    far_sent = far_pack(raw, token)
    far_strip = lax.ppermute(far_sent, "tm", far_pairs)
    near_sent, inner_taps, far_taps, near_taps = near_pack(raw, far_sent, band_taps, early)
    near_strip = lax.ppermute(near_sent, "tm", near_pairs)
    gains, onehot = channel_tables(
        band_gain, band_taps, gain_index.T, owner_of.reshape(-1, LANES), seat.reshape(-1, LANES), cables
    )
    inner_sums = window(
        inner_kernel, "inner_window", jax.ShapeDtypeStruct((cables, INNER), F32), [], 1,
        (raw, inner_taps, gains, onehot),
    )
    others = window(
        near_kernel, "near_window", jax.ShapeDtypeStruct((cables, depth), F32), [], 2,
        (raw, near_strip, near_taps, gains, onehot, inner_sums),
    )
    pitch = -(-(depth // LANES) * cab_dev // 8) * 8
    parts = window(
        far_kernel, "far_window", jax.ShapeDtypeStruct((chan_count, pitch, LANES), BF16),
        [pltpu.VMEM((chan_count * pitch, LANES), F32)], 2,
        (raw, far_strip, far_taps, gains, onehot, others),
    )
    parts = lax.all_to_all(parts, "chan", split_axis=0, concat_axis=0, tiled=True)
    return finish(parts, cable_length, depth)


def solution(mesh):
    return jax.shard_map(
        shards,
        mesh=mesh,
        in_specs=(P("chan", "tm"), P(), P(), P("chan", None), P(), P(), P("chan")),
        out_specs=P("chan", "tm"),
        check_vma=False,
    )
```

```python
import jax
import jax.numpy as jnp
from jax import lax
from jax.experimental import pallas as pl
from jax.experimental.pallas import tpu as pltpu
from jax.sharding import PartitionSpec as P

LANES = 128
SIDE = 144
INNER = 256
SIDE_COLS = 2048
INNER_COLS = 2048
F32 = jnp.float32
BF16 = jnp.bfloat16
NT = (((1,), (1,)), ((), ()))


def beside_rows(beside, lane_at):
    count = beside.shape[0]
    lane = lax.broadcasted_iota(jnp.int32, (16, LANES), 1)
    pick = (lane == lane_at).astype(F32).astype(BF16)
    column = lax.dot_general(pick, beside, NT, preferred_element_type=F32)
    rows = [column[0:1, a * LANES : (a + 1) * LANES] for a in range(count // LANES)]
    return jnp.concatenate(rows, axis=0).astype(BF16)


def is_low_core():
    return lax.axis_index("tm") % 2 == 0


def fill_strip(side, raw_ref, strip_ref):
    count = raw_ref.shape[0]
    strip_ref[0:count, :] = raw_ref[:, pl.ds(pl.multiple_of(side * (3 * LANES), LANES), LANES)]
    beside = raw_ref[:, pl.ds(pl.multiple_of(LANES + side * LANES, LANES), LANES)]
    strip_ref[count:, :] = beside_rows(beside, side * (LANES - 1))


def first_kernel(
    raw_ref, taps_ref, strip_ref, inner_taps_ref, far_taps_ref, near_taps_ref, beside, taps, sems
):
    side = lax.axis_index("tm") % 2
    count = raw_ref.shape[0]
    at = pl.multiple_of(side * (3 * LANES), LANES)
    by = pl.multiple_of(LANES + side * LANES, LANES)
    jobs = [
        pltpu.make_async_copy(raw_ref.at[:, pl.ds(by, LANES)], beside, sems.at[0]),
        pltpu.make_async_copy(raw_ref.at[:, pl.ds(at, LANES)], strip_ref.at[0:count], sems.at[1]),
    ]
    for job in jobs:
        job.start()

    @pl.when(side == 1)
    def _():
        job = pltpu.make_async_copy(taps_ref, taps, sems.at[2])
        job.start()
        job.wait()
        build_taps(False, taps, inner_taps_ref, far_taps_ref, near_taps_ref)

    jobs[0].wait()
    strip_ref[count:, :] = beside_rows(beside[...], side * (LANES - 1))
    jobs[1].wait()


def near_pack_kernel(
    raw_ref, after_ref, taps_ref, early_inner_ref, early_far_ref, early_near_ref,
    strip_ref, inner_taps_ref, far_taps_ref, near_taps_ref,
):
    del after_ref
    fill_strip(1 - lax.axis_index("tm") % 2, raw_ref, strip_ref)

    @pl.when(is_low_core())
    def _():
        build_taps(True, taps_ref, inner_taps_ref, far_taps_ref, near_taps_ref)

    @pl.when(jnp.logical_not(is_low_core()))
    def _():
        inner_taps_ref[...] = early_inner_ref[...]
        far_taps_ref[...] = early_far_ref[...]
        near_taps_ref[...] = early_near_ref[...]


def first(raw, taps):
    count, depth = raw.shape
    outs = [jax.ShapeDtypeStruct((count + 16, LANES), BF16)] + tap_shapes(taps, depth)
    return pl.pallas_call(
        first_kernel,
        in_specs=[pl.BlockSpec(memory_space=pltpu.HBM)] * 2,
        out_specs=[pl.BlockSpec(memory_space=pltpu.VMEM)] * len(outs),
        out_shape=outs,
        scratch_shapes=[
            pltpu.VMEM((count, LANES), BF16),
            pltpu.VMEM(taps.shape, F32),
            pltpu.SemaphoreType.DMA((3,)),
        ],
        compiler_params=pltpu.CompilerParams(vmem_limit_bytes=16 << 20),
        name="far_strip",
    )(*[pltpu.with_memory_space_constraint(a, pltpu.HBM) for a in (raw, taps)])


def near_pack(raw, after, taps, early):
    count, depth = raw.shape
    vmem = pl.BlockSpec(memory_space=pltpu.VMEM)
    return pl.pallas_call(
        near_pack_kernel,
        in_specs=[vmem, pl.BlockSpec(memory_space=pl.ANY)] + [vmem] * 4,
        out_specs=[vmem] * 4,
        out_shape=[jax.ShapeDtypeStruct((count + 16, LANES), BF16)] + tap_shapes(taps, depth),
        compiler_params=pltpu.CompilerParams(vmem_limit_bytes=8 << 20),
        cost_estimate=pl.CostEstimate(
            flops=2 * count * depth * 768, bytes_accessed=4 << 20, transcendentals=0
        ),
        name="near_strip",
    )(raw, after, taps, *early)


def window_sums(columns_of, taps_ref, size, gains_ref, edges_of, onehot_ref, count, step):
    sub = lax.broadcasted_iota(jnp.int32, (8, step), 0)
    total = None
    for start in range(0, count, step):
        part = slice(start, start + step)
        bands = lax.dot_general(taps_ref[...], columns_of(part), NT, preferred_element_type=F32)
        held = gains_ref[0:1, part] * bands[0:size]
        for b in (1, 2):
            held = held + gains_ref[b : b + 1, part] * bands[b * size : (b + 1) * size]
        first, last = held[0:8], held[size - 8 : size]
        if edges_of is not None:
            low, high = edges_of(start)
            first = first + jnp.where(sub == 0, low, 0.0)
            last = last + jnp.where(sub == 7, high, 0.0)
        middle = held[8 : size - 8]
        ahead = jnp.concatenate([middle, last, pltpu.roll(first, 7, 0)], axis=0)
        behind = jnp.concatenate([pltpu.roll(last, 1, 0), first, middle], axis=0)
        rate = (ahead - behind).astype(BF16)
        power = rate * jnp.abs(rate)
        term = lax.dot_general(onehot_ref[:, part], power, NT, preferred_element_type=F32)
        total = term if total is None else total + term
    return total


def sample_of_row(rows, size, cols):
    row = lax.broadcasted_iota(jnp.int32, (rows, cols), 0)
    return jnp.bitwise_and(row, 7) * (size // 8) + jnp.right_shift(row, 3)


def build_taps(is_low, taps_ref, inner_taps_ref, far_taps_ref, near_taps_ref):
    tm_pos = lax.axis_index("tm")
    inside = jnp.logical_and(tm_pos > 0, tm_pos < lax.axis_size("tm") - 1).astype(F32)
    depth = inner_taps_ref.shape[1]
    bands, width = taps_ref.shape
    wide = depth + LANES

    reach = 3 * LANES
    lane = lax.broadcasted_iota(jnp.int32, (bands, reach - 2 * LANES), 1)
    tail = jnp.where(lane == 0, taps_ref[:, width - 1 : width], 0.0)
    taps = jnp.concatenate([taps_ref[:, 0 : width - 1], tail], axis=1).astype(BF16)
    turn = (
        lax.broadcasted_iota(jnp.int32, (reach, wide), 0) + lax.broadcasted_iota(jnp.int32, (reach, wide), 1)
        == width - 1
    )
    base = jnp.dot(taps, turn.astype(F32).astype(BF16), preferred_element_type=F32)
    sub = lax.broadcasted_iota(jnp.int32, (8, depth), 0)

    row = lax.broadcasted_iota(jnp.int32, (8, wide), 0)

    def rows_of(b, size, shifts):
        line = jnp.broadcast_to(base[b : b + 1, :], (8, wide))
        spread = size // 8
        fan = line
        for i in range(1, 8):
            fan = jnp.where(row == i, pltpu.roll(line, i * spread, 1), fan)
        return [
            [pltpu.roll(fan, (j + shift) % wide, 1)[:, 0:depth] for j in range(spread)]
            for shift in shifts
        ]

    for b in range(bands):
        (rows,) = rows_of(b, INNER, (0,))
        for j in range(0, INNER // 8, 2):
            at = b * INNER + 8 * j
            inner_taps_ref[at : at + 16, :] = jnp.concatenate(rows[j : j + 2], axis=0).astype(BF16)
        low, high = rows_of(b, SIDE, (-1, 2 * LANES + 1 - SIDE))
        if is_low:
            low[0] = jnp.where(sub == 0, low[0] * inside, low[0])
        else:
            high[-1] = jnp.where(sub == 7, high[-1] * inside, high[-1])
        for j in range(0, SIDE // 8, 2):
            at = slice(b * SIDE + 8 * j, b * SIDE + 8 * j + 16)
            low_rows = jnp.concatenate(low[j : j + 2], axis=0).astype(BF16)
            high_rows = jnp.concatenate(high[j : j + 2], axis=0).astype(BF16)
            high_rows = jnp.concatenate([high_rows[:, 3 * LANES :], high_rows[:, : 3 * LANES]], axis=1)

            far_taps_ref[at, :], near_taps_ref[at, :] = (
                (low_rows, high_rows) if is_low else (high_rows, low_rows)
            )


def tap_shapes(taps, depth):
    rows = (INNER, SIDE, SIDE)
    return [jax.ShapeDtypeStruct((taps.shape[0] * r, depth), BF16) for r in rows]


def channels_kernel(
    levels_ref, length_ref, taps_ref, index_ref, owner_ref, seat_ref, gains_ref, onehot_ref, divisor_ref
):
    is_low = is_low_core()
    bands, width = taps_ref.shape
    blocks = index_ref.shape[1] // LANES
    index = index_ref[...]
    gains = jnp.zeros(index.shape, F32)
    for level in range(levels_ref.shape[0]):
        gains = jnp.where(index == level, levels_ref[level], gains)
    gains = 0.5 * gains
    first = taps_ref[:, 0:1].astype(BF16).astype(F32)
    final = taps_ref[:, width - 1 : width].astype(BF16).astype(F32)
    low_edge = jnp.sum(gains * final, axis=0, keepdims=True)
    high_edge = jnp.sum(gains * first, axis=0, keepdims=True)
    gains_ref[0:bands, :] = gains
    gains_ref[3:4, :] = jnp.where(is_low, low_edge, high_edge)
    gains_ref[4:5, :] = jnp.where(is_low, high_edge, low_edge)
    mine = pl.ds(pl.multiple_of(lax.axis_index("chan") * blocks, blocks), blocks)
    place = seat_ref[mine, :] * lax.axis_size("chan") + owner_ref[mine, :]
    cable = lax.broadcasted_iota(jnp.int32, (onehot_ref.shape[0], LANES), 0)
    for a in range(blocks):
        onehot_ref[:, a * LANES : (a + 1) * LANES] = (cable == place[a : a + 1, :]).astype(F32).astype(BF16)
    tiles = divisor_ref.shape[0] // length_ref.shape[0]
    divisor_ref[...] = jnp.ones_like(divisor_ref)
    for k in range(length_ref.shape[0]):
        divisor_ref[k * tiles : (k + 1) * tiles, :] = jnp.full((tiles, LANES), length_ref[k].astype(F32))


def channel_tables(band_gain, cable_length, taps, index, owner, seat, cables, pitch):
    count = index.shape[1]
    vmem = pl.BlockSpec(memory_space=pltpu.VMEM)
    return pl.pallas_call(
        channels_kernel,
        in_specs=[pl.BlockSpec(memory_space=pltpu.SMEM)] * 2 + [vmem] * 4,
        out_specs=[vmem] * 3,
        out_shape=[
            jax.ShapeDtypeStruct((8, count), F32),
            jax.ShapeDtypeStruct((cables, count), BF16),
            jax.ShapeDtypeStruct((pitch, LANES), F32),
        ],
        compiler_params=pltpu.CompilerParams(vmem_limit_bytes=8 << 20),
        cost_estimate=pl.CostEstimate(flops=1 << 30, bytes_accessed=1 << 20, transcendentals=0),
        name="channel_tables",
    )(band_gain, cable_length, taps, index, owner, seat)


def inner_kernel(raw_ref, taps_ref, gains_ref, onehot_ref, sums_ref):
    count = raw_ref.shape[0]
    sums_ref[...] = window_sums(
        lambda part: raw_ref[part, :], taps_ref, INNER, gains_ref, None, onehot_ref, count, INNER_COLS
    )


def side_sums(is_low, edge_row, raw_ref, strip_ref, taps_ref, gains_ref, onehot_ref):
    count = raw_ref.shape[0]
    offset = pl.multiple_of(jnp.where(is_low, 0, LANES), LANES)
    beside = strip_ref[count:, :].astype(F32)

    def columns_of(part):
        return jnp.concatenate([strip_ref[part, :], raw_ref[part, pl.ds(offset, 3 * LANES)]], axis=1)

    def edges_of(start):
        rows = range(start // LANES, (start + SIDE_COLS) // LANES)
        line = jnp.concatenate([beside[a : a + 1, :] for a in rows], axis=1)
        line = line * gains_ref[edge_row : edge_row + 1, start : start + SIDE_COLS]
        return jnp.where(is_low, line, 0.0), jnp.where(is_low, 0.0, line)

    sums = window_sums(
        columns_of, taps_ref, SIDE, gains_ref, edges_of, onehot_ref, count, SIDE_COLS
    )
    depth = raw_ref.shape[1]
    sample = sample_of_row(SIDE, SIDE, depth)
    sample = sample + jnp.where(is_low, -1, depth + 1 - SIDE)
    kept = (sample >= jnp.where(is_low, 0, depth - 1 - LANES)) & (
        sample <= jnp.where(is_low, LANES, depth - 1)
    )
    col = lax.broadcasted_iota(jnp.int32, (SIDE, depth), 1)
    order = ((col == sample) & kept).astype(F32).astype(BF16)
    return jnp.dot(sums.astype(BF16), order, preferred_element_type=F32)


def near_kernel(raw_ref, strip_ref, taps_ref, gains_ref, onehot_ref, inner_ref, sums_ref):
    near = side_sums(jnp.logical_not(is_low_core()), 4, raw_ref, strip_ref, taps_ref, gains_ref, onehot_ref)
    depth = raw_ref.shape[1]
    sample = sample_of_row(INNER, INNER, depth) + LANES
    kept = (sample > LANES) & (sample < depth - LANES - 1)
    col = lax.broadcasted_iota(jnp.int32, (INNER, depth), 1)
    order = ((col == sample) & kept).astype(F32).astype(BF16)
    sums_ref[...] = near + jnp.dot(inner_ref[...].astype(BF16), order, preferred_element_type=F32)


def far_kernel(
    raw_ref, strip_ref, taps_ref, gains_ref, onehot_ref, others_ref, out_ref, scr
):
    owners, pitch, _ = out_ref.shape
    seats = others_ref.shape[0] // owners
    far = side_sums(is_low_core(), 3, raw_ref, strip_ref, taps_ref, gains_ref, onehot_ref)
    sums = others_ref[...] + far
    tiles = sums.shape[1] // LANES
    for spare in range(tiles * seats, pitch):
        scr[pl.ds(spare, owners, stride=pitch), :] = jnp.zeros((owners, LANES), F32)
    for s in range(seats):
        for j in range(tiles):
            scr[pl.ds(tiles * s + j, owners, stride=pitch), :] = sums[
                s * owners : (s + 1) * owners, j * LANES : (j + 1) * LANES
            ]
    for o in range(owners):
        out_ref[o, :, :] = scr[o * pitch : (o + 1) * pitch, :].astype(BF16)


def window(kernel, name, out_shape, scratch, taps_at, args):
    count, depth = args[0].shape
    vmem = pl.BlockSpec(memory_space=pltpu.VMEM)
    return pl.pallas_call(
        kernel,
        in_specs=[vmem] * len(args),
        out_specs=vmem,
        out_shape=out_shape,
        scratch_shapes=scratch,
        compiler_params=pltpu.CompilerParams(vmem_limit_bytes=24 << 20),
        cost_estimate=pl.CostEstimate(
            flops=(50 if name == 'inner_window' else 1) * 2 * count * depth * 768, bytes_accessed=4<<20, transcendentals=0
        ),
        name=name,
    )(*args)


def finish_kernel(divisor_ref, parts_ref, out_ref):
    seats, depth = out_ref.shape
    tiles = depth // LANES
    total = jnp.sum(parts_ref[...].astype(F32), axis=0) / divisor_ref[...]
    for s in range(seats):
        for j in range(tiles):
            row = tiles * s + j
            out_ref[s : s + 1, j * LANES : (j + 1) * LANES] = total[row : row + 1]


def finish(parts, divisor, seats, depth):
    vmem = pl.BlockSpec(memory_space=pltpu.VMEM)
    return pl.pallas_call(
        finish_kernel,
        in_specs=[vmem, vmem],
        out_specs=vmem,
        out_shape=jax.ShapeDtypeStruct((seats, depth), F32),
        compiler_params=pltpu.CompilerParams(vmem_limit_bytes=4 << 20),
        name="finish_sum",
    )(divisor, parts)


def shards(raw, band_taps, band_gain, gain_index, owner_of, seat, cable_length):
    tm_count = lax.axis_size("tm")
    chan_count = lax.axis_size("chan")
    depth = raw.shape[1]
    far_pairs = [(i, i + 1) for i in range(1, tm_count - 1, 2)]
    far_pairs = far_pairs + [(j, i) for i, j in far_pairs]
    near_pairs = [(i, i ^ 1) for i in range(tm_count)]
    cab_dev = cable_length.shape[0]
    cables = cab_dev * chan_count

    far_sent, *early = first(raw, band_taps)
    far_strip = lax.ppermute(far_sent, "tm", far_pairs)
    near_sent, inner_taps, far_taps, near_taps = near_pack(raw, far_sent, band_taps, early)
    near_strip = lax.ppermute(near_sent, "tm", near_pairs)
    pitch = -(-(depth // LANES) * cab_dev // 8) * 8
    gains, onehot, divisor = channel_tables(
        band_gain, cable_length, band_taps, gain_index.T,
        owner_of.reshape(-1, LANES), seat.reshape(-1, LANES), cables, pitch,
    )
    inner_sums = window(
        inner_kernel, "inner_window", jax.ShapeDtypeStruct((cables, INNER), F32), [], 1,
        (raw, inner_taps, gains, onehot),
    )
    others = window(
        near_kernel, "near_window", jax.ShapeDtypeStruct((cables, depth), F32), [], 2,
        (raw, near_strip, near_taps, gains, onehot, inner_sums),
    )
    parts = window(
        far_kernel, "far_window", jax.ShapeDtypeStruct((chan_count, pitch, LANES), BF16),
        [pltpu.VMEM((chan_count * pitch, LANES), F32)], 2,
        (raw, far_strip, far_taps, gains, onehot, others),
    )
    parts = lax.all_to_all(parts, "chan", split_axis=0, concat_axis=0, tiled=True)
    return finish(parts, divisor, cab_dev, depth)


def solution(mesh):
    return jax.shard_map(
        shards,
        mesh=mesh,
        in_specs=(P("chan", "tm"), P(), P(), P("chan", None), P(), P(), P("chan")),
        out_specs=P("chan", "tm"),
        check_vma=False,
    )
```

```python
import jax
import jax.numpy as jnp
from jax import lax
from jax.experimental import pallas as pl
from jax.experimental.pallas import tpu as pltpu
from jax.sharding import PartitionSpec as P

LANES = 128
SIDE = 144
INNER = 256
SIDE_COLS = 2048
INNER_COLS = 2048
F32 = jnp.float32
BF16 = jnp.bfloat16
NT = (((1,), (1,)), ((), ()))


def beside_rows(beside, lane_at):
    count = beside.shape[0]
    lane = lax.broadcasted_iota(jnp.int32, (16, LANES), 1)
    pick = (lane == lane_at).astype(F32).astype(BF16)
    column = lax.dot_general(pick, beside, NT, preferred_element_type=F32)
    rows = [column[0:1, a * LANES : (a + 1) * LANES] for a in range(count // LANES)]
    return jnp.concatenate(rows, axis=0).astype(BF16)


def is_low_core():
    return lax.axis_index("tm") % 2 == 0


def fill_strip(side, raw_ref, strip_ref):
    count = raw_ref.shape[0]
    strip_ref[0:count, :] = raw_ref[:, pl.ds(pl.multiple_of(side * (3 * LANES), LANES), LANES)]
    beside = raw_ref[:, pl.ds(pl.multiple_of(LANES + side * LANES, LANES), LANES)]
    strip_ref[count:, :] = beside_rows(beside, side * (LANES - 1))


def first_kernel(
    raw_ref, taps_ref, strip_ref, inner_taps_ref, far_taps_ref, near_taps_ref, beside, taps, sems
):
    side = lax.axis_index("tm") % 2
    count = raw_ref.shape[0]
    at = pl.multiple_of(side * (3 * LANES), LANES)
    by = pl.multiple_of(LANES + side * LANES, LANES)
    jobs = [
        pltpu.make_async_copy(raw_ref.at[:, pl.ds(by, LANES)], beside, sems.at[0]),
        pltpu.make_async_copy(raw_ref.at[:, pl.ds(at, LANES)], strip_ref.at[0:count], sems.at[1]),
    ]
    for job in jobs:
        job.start()

    @pl.when(side == 1)
    def _():
        job = pltpu.make_async_copy(taps_ref, taps, sems.at[2])
        job.start()
        job.wait()
        build_taps(False, taps, inner_taps_ref, far_taps_ref, near_taps_ref)

    jobs[0].wait()
    strip_ref[count:, :] = beside_rows(beside[...], side * (LANES - 1))
    jobs[1].wait()


def near_pack_kernel(
    raw_ref, after_ref, taps_ref, early_inner_ref, early_far_ref, early_near_ref,
    strip_ref, inner_taps_ref, far_taps_ref, near_taps_ref,
):
    del after_ref
    fill_strip(1 - lax.axis_index("tm") % 2, raw_ref, strip_ref)

    @pl.when(is_low_core())
    def _():
        build_taps(True, taps_ref, inner_taps_ref, far_taps_ref, near_taps_ref)

    @pl.when(jnp.logical_not(is_low_core()))
    def _():
        inner_taps_ref[...] = early_inner_ref[...]
        far_taps_ref[...] = early_far_ref[...]
        near_taps_ref[...] = early_near_ref[...]


def first(raw, taps):
    count, depth = raw.shape
    outs = [jax.ShapeDtypeStruct((count + 16, LANES), BF16)] + tap_shapes(taps, depth)
    return pl.pallas_call(
        first_kernel,
        in_specs=[pl.BlockSpec(memory_space=pltpu.HBM)] * 2,
        out_specs=[pl.BlockSpec(memory_space=pltpu.VMEM)] * len(outs),
        out_shape=outs,
        scratch_shapes=[
            pltpu.VMEM((count, LANES), BF16),
            pltpu.VMEM(taps.shape, F32),
            pltpu.SemaphoreType.DMA((3,)),
        ],
        compiler_params=pltpu.CompilerParams(vmem_limit_bytes=16 << 20),
        name="far_strip",
    )(*[pltpu.with_memory_space_constraint(a, pltpu.HBM) for a in (raw, taps)])


def near_pack(raw, after, taps, early):
    count, depth = raw.shape
    vmem = pl.BlockSpec(memory_space=pltpu.VMEM)
    return pl.pallas_call(
        near_pack_kernel,
        in_specs=[vmem, pl.BlockSpec(memory_space=pl.ANY)] + [vmem] * 4,
        out_specs=[vmem] * 4,
        out_shape=[jax.ShapeDtypeStruct((count + 16, LANES), BF16)] + tap_shapes(taps, depth),
        compiler_params=pltpu.CompilerParams(vmem_limit_bytes=8 << 20),
        cost_estimate=pl.CostEstimate(
            flops=2 * count * depth * 768, bytes_accessed=4 << 20, transcendentals=0
        ),
        name="near_strip",
    )(raw, after, taps, *early)


def window_sums(columns_of, taps_ref, size, gains_ref, edges_of, onehot_ref, count, step):
    sub = lax.broadcasted_iota(jnp.int32, (8, step), 0)
    total = None
    for start in range(0, count, step):
        part = slice(start, start + step)
        bands = lax.dot_general(taps_ref[...], columns_of(part), NT, preferred_element_type=F32)
        held = gains_ref[0:1, part] * bands[0:size]
        for b in (1, 2):
            held = held + gains_ref[b : b + 1, part] * bands[b * size : (b + 1) * size]
        first, last = held[0:8], held[size - 8 : size]
        if edges_of is not None:
            low, high = edges_of(start)
            first = first + jnp.where(sub == 0, low, 0.0)
            last = last + jnp.where(sub == 7, high, 0.0)
        middle = held[8 : size - 8]
        ahead = jnp.concatenate([middle, last, pltpu.roll(first, 7, 0)], axis=0)
        behind = jnp.concatenate([pltpu.roll(last, 1, 0), first, middle], axis=0)
        rate = (ahead - behind).astype(BF16)
        power = rate * jnp.abs(rate)
        term = lax.dot_general(onehot_ref[:, part], power, NT, preferred_element_type=F32)
        total = term if total is None else total + term
    return total


def sample_of_row(rows, size, cols):
    row = lax.broadcasted_iota(jnp.int32, (rows, cols), 0)
    return jnp.bitwise_and(row, 7) * (size // 8) + jnp.right_shift(row, 3)


def build_taps(is_low, taps_ref, inner_taps_ref, far_taps_ref, near_taps_ref):
    tm_pos = lax.axis_index("tm")
    inside = jnp.logical_and(tm_pos > 0, tm_pos < lax.axis_size("tm") - 1).astype(F32)
    depth = inner_taps_ref.shape[1]
    bands, width = taps_ref.shape
    wide = depth + LANES

    reach = 3 * LANES
    lane = lax.broadcasted_iota(jnp.int32, (bands, reach - 2 * LANES), 1)
    tail = jnp.where(lane == 0, taps_ref[:, width - 1 : width], 0.0)
    taps = jnp.concatenate([taps_ref[:, 0 : width - 1], tail], axis=1).astype(BF16)
    turn = (
        lax.broadcasted_iota(jnp.int32, (reach, wide), 0) + lax.broadcasted_iota(jnp.int32, (reach, wide), 1)
        == width - 1
    )
    base = jnp.dot(taps, turn.astype(F32).astype(BF16), preferred_element_type=F32)
    sub = lax.broadcasted_iota(jnp.int32, (8, depth), 0)

    row = lax.broadcasted_iota(jnp.int32, (8, wide), 0)

    def rows_of(b, size, shifts):
        line = jnp.broadcast_to(base[b : b + 1, :], (8, wide))
        spread = size // 8
        fan = line
        for i in range(1, 8):
            fan = jnp.where(row == i, pltpu.roll(line, i * spread, 1), fan)
        return [
            [pltpu.roll(fan, (j + shift) % wide, 1)[:, 0:depth] for j in range(spread)]
            for shift in shifts
        ]

    for b in range(bands):
        (rows,) = rows_of(b, INNER, (0,))
        for j in range(0, INNER // 8, 2):
            at = b * INNER + 8 * j
            inner_taps_ref[at : at + 16, :] = jnp.concatenate(rows[j : j + 2], axis=0).astype(BF16)
        low, high = rows_of(b, SIDE, (-1, 2 * LANES + 1 - SIDE))
        if is_low:
            low[0] = jnp.where(sub == 0, low[0] * inside, low[0])
        else:
            high[-1] = jnp.where(sub == 7, high[-1] * inside, high[-1])
        for j in range(0, SIDE // 8, 2):
            at = slice(b * SIDE + 8 * j, b * SIDE + 8 * j + 16)
            low_rows = jnp.concatenate(low[j : j + 2], axis=0).astype(BF16)
            high_rows = jnp.concatenate(high[j : j + 2], axis=0).astype(BF16)
            high_rows = jnp.concatenate([high_rows[:, 3 * LANES :], high_rows[:, : 3 * LANES]], axis=1)

            far_taps_ref[at, :], near_taps_ref[at, :] = (
                (low_rows, high_rows) if is_low else (high_rows, low_rows)
            )


def tap_shapes(taps, depth):
    rows = (INNER, SIDE, SIDE)
    return [jax.ShapeDtypeStruct((taps.shape[0] * r, depth), BF16) for r in rows]


def inner_kernel(
    levels_ref, length_ref, raw_ref, inner_taps_ref, taps_ref, index_ref, owner_ref, seat_ref,
    sums_ref, gains_ref, onehot_ref, divisor_ref,
):
    is_low = is_low_core()
    bands, width = taps_ref.shape
    blocks = index_ref.shape[1] // LANES
    index = index_ref[...]
    gains = jnp.zeros(index.shape, F32)
    for level in range(levels_ref.shape[0]):
        gains = jnp.where(index == level, levels_ref[level], gains)
    gains = 0.5 * gains
    first = taps_ref[:, 0:1].astype(BF16).astype(F32)
    final = taps_ref[:, width - 1 : width].astype(BF16).astype(F32)
    low_edge = jnp.sum(gains * final, axis=0, keepdims=True)
    high_edge = jnp.sum(gains * first, axis=0, keepdims=True)
    gains_ref[0:bands, :] = gains
    gains_ref[3:4, :] = jnp.where(is_low, low_edge, high_edge)
    gains_ref[4:5, :] = jnp.where(is_low, high_edge, low_edge)
    mine = pl.ds(pl.multiple_of(lax.axis_index("chan") * blocks, blocks), blocks)
    place = seat_ref[mine, :] * lax.axis_size("chan") + owner_ref[mine, :]
    cable = lax.broadcasted_iota(jnp.int32, (onehot_ref.shape[0], LANES), 0)
    for a in range(blocks):
        onehot_ref[:, a * LANES : (a + 1) * LANES] = (cable == place[a : a + 1, :]).astype(F32).astype(BF16)
    tiles = divisor_ref.shape[0] // length_ref.shape[0]
    divisor_ref[...] = jnp.ones_like(divisor_ref)
    for k in range(length_ref.shape[0]):
        divisor_ref[k * tiles : (k + 1) * tiles, :] = jnp.full((tiles, LANES), length_ref[k].astype(F32))
    count = raw_ref.shape[0]
    sums_ref[...] = window_sums(
        lambda part: raw_ref[part, :], inner_taps_ref, INNER, gains_ref, None, onehot_ref, count, INNER_COLS
    )


def side_sums(is_low, edge_row, raw_ref, strip_ref, taps_ref, gains_ref, onehot_ref):
    count = raw_ref.shape[0]
    offset = pl.multiple_of(jnp.where(is_low, 0, LANES), LANES)
    beside = strip_ref[count:, :].astype(F32)

    def columns_of(part):
        return jnp.concatenate([strip_ref[part, :], raw_ref[part, pl.ds(offset, 3 * LANES)]], axis=1)

    def edges_of(start):
        rows = range(start // LANES, (start + SIDE_COLS) // LANES)
        line = jnp.concatenate([beside[a : a + 1, :] for a in rows], axis=1)
        line = line * gains_ref[edge_row : edge_row + 1, start : start + SIDE_COLS]
        return jnp.where(is_low, line, 0.0), jnp.where(is_low, 0.0, line)

    sums = window_sums(
        columns_of, taps_ref, SIDE, gains_ref, edges_of, onehot_ref, count, SIDE_COLS
    )
    depth = raw_ref.shape[1]
    sample = sample_of_row(SIDE, SIDE, depth)
    sample = sample + jnp.where(is_low, -1, depth + 1 - SIDE)
    kept = (sample >= jnp.where(is_low, 0, depth - 1 - LANES)) & (
        sample <= jnp.where(is_low, LANES, depth - 1)
    )
    col = lax.broadcasted_iota(jnp.int32, (SIDE, depth), 1)
    order = ((col == sample) & kept).astype(F32).astype(BF16)
    return jnp.dot(sums.astype(BF16), order, preferred_element_type=F32)


def near_kernel(raw_ref, strip_ref, taps_ref, gains_ref, onehot_ref, inner_ref, sums_ref):
    near = side_sums(jnp.logical_not(is_low_core()), 4, raw_ref, strip_ref, taps_ref, gains_ref, onehot_ref)
    depth = raw_ref.shape[1]
    sample = sample_of_row(INNER, INNER, depth) + LANES
    kept = (sample > LANES) & (sample < depth - LANES - 1)
    col = lax.broadcasted_iota(jnp.int32, (INNER, depth), 1)
    order = ((col == sample) & kept).astype(F32).astype(BF16)
    sums_ref[...] = near + jnp.dot(inner_ref[...].astype(BF16), order, preferred_element_type=F32)


def far_kernel(
    raw_ref, strip_ref, taps_ref, gains_ref, onehot_ref, others_ref, out_ref, scr
):
    owners, pitch, _ = out_ref.shape
    seats = others_ref.shape[0] // owners
    far = side_sums(is_low_core(), 3, raw_ref, strip_ref, taps_ref, gains_ref, onehot_ref)
    sums = others_ref[...] + far
    tiles = sums.shape[1] // LANES
    for spare in range(tiles * seats, pitch):
        scr[pl.ds(spare, owners, stride=pitch), :] = jnp.zeros((owners, LANES), F32)
    for s in range(seats):
        for j in range(tiles):
            scr[pl.ds(tiles * s + j, owners, stride=pitch), :] = sums[
                s * owners : (s + 1) * owners, j * LANES : (j + 1) * LANES
            ]
    for o in range(owners):
        out_ref[o, :, :] = scr[o * pitch : (o + 1) * pitch, :].astype(BF16)


def window(kernel, name, out_shape, scratch, flops, args, scalars=()):
    smem = pl.BlockSpec(memory_space=pltpu.SMEM)
    vmem = pl.BlockSpec(memory_space=pltpu.VMEM)
    many = isinstance(out_shape, list)
    return pl.pallas_call(
        kernel,
        in_specs=[smem] * len(scalars) + [vmem] * len(args),
        out_specs=[vmem] * len(out_shape) if many else vmem,
        out_shape=out_shape,
        scratch_shapes=scratch,
        compiler_params=pltpu.CompilerParams(vmem_limit_bytes=24 << 20),
        cost_estimate=pl.CostEstimate(flops=flops, bytes_accessed=4 << 20, transcendentals=0),
        name=name,
    )(*scalars, *args)


def finish_kernel(divisor_ref, parts_ref, out_ref):
    seats, depth = out_ref.shape
    tiles = depth // LANES
    total = jnp.sum(parts_ref[...].astype(F32), axis=0) / divisor_ref[...]
    for s in range(seats):
        for j in range(tiles):
            row = tiles * s + j
            out_ref[s : s + 1, j * LANES : (j + 1) * LANES] = total[row : row + 1]


def finish(parts, divisor, seats, depth):
    vmem = pl.BlockSpec(memory_space=pltpu.VMEM)
    return pl.pallas_call(
        finish_kernel,
        in_specs=[vmem, vmem],
        out_specs=vmem,
        out_shape=jax.ShapeDtypeStruct((seats, depth), F32),
        compiler_params=pltpu.CompilerParams(vmem_limit_bytes=4 << 20),
        name="finish_sum",
    )(divisor, parts)


def shards(raw, band_taps, band_gain, gain_index, owner_of, seat, cable_length):
    tm_count = lax.axis_size("tm")
    chan_count = lax.axis_size("chan")
    depth = raw.shape[1]
    far_pairs = [(i, i + 1) for i in range(1, tm_count - 1, 2)]
    far_pairs = far_pairs + [(j, i) for i, j in far_pairs]
    near_pairs = [(i, i ^ 1) for i in range(tm_count)]
    cab_dev = cable_length.shape[0]
    cables = cab_dev * chan_count

    far_sent, *early = first(raw, band_taps)
    far_strip = lax.ppermute(far_sent, "tm", far_pairs)
    near_sent, inner_taps, far_taps, near_taps = near_pack(raw, far_sent, band_taps, early)
    near_strip = lax.ppermute(near_sent, "tm", near_pairs)
    pitch = -(-(depth // LANES) * cab_dev // 8) * 8
    work = 2 * raw.shape[0] * depth * inner_taps.shape[0]
    inner_sums, gains, onehot, divisor = window(
        inner_kernel, "inner_window",
        [
            jax.ShapeDtypeStruct((cables, INNER), F32),
            jax.ShapeDtypeStruct((8, raw.shape[0]), F32),
            jax.ShapeDtypeStruct((cables, raw.shape[0]), BF16),
            jax.ShapeDtypeStruct((pitch, LANES), F32),
        ],
        [], 50 * work,
        (
            raw, inner_taps, band_taps, gain_index.T,
            owner_of.reshape(-1, LANES), seat.reshape(-1, LANES),
        ),
        (band_gain, cable_length),
    )
    others = window(
        near_kernel, "near_window", jax.ShapeDtypeStruct((cables, depth), F32), [], work,
        (raw, near_strip, near_taps, gains, onehot, inner_sums),
    )
    parts = window(
        far_kernel, "far_window", jax.ShapeDtypeStruct((chan_count, pitch, LANES), BF16),
        [pltpu.VMEM((chan_count * pitch, LANES), F32)], work,
        (raw, far_strip, far_taps, gains, onehot, others),
    )
    parts = lax.all_to_all(parts, "chan", split_axis=0, concat_axis=0, tiled=True)
    return finish(parts, divisor, cab_dev, depth)


def solution(mesh):
    return jax.shard_map(
        shards,
        mesh=mesh,
        in_specs=(P("chan", "tm"), P(), P(), P("chan", None), P(), P(), P("chan")),
        out_specs=P("chan", "tm"),
        check_vma=False,
    )
```

```python
import jax
import jax.numpy as jnp
from jax import lax
from jax.experimental import pallas as pl
from jax.experimental.pallas import tpu as pltpu
from jax.sharding import PartitionSpec as P

LANES = 128
SIDE = 144
INNER = 256
SIDE_COLS = 2048
INNER_COLS = 2048
F32 = jnp.float32
BF16 = jnp.bfloat16
NT = (((1,), (1,)), ((), ()))


def beside_rows(beside, lane_at):
    count = beside.shape[0]
    lane = lax.broadcasted_iota(jnp.int32, (16, LANES), 1)
    pick = (lane == lane_at).astype(F32).astype(BF16)
    column = lax.dot_general(pick, beside, NT, preferred_element_type=F32)
    rows = [column[0:1, a * LANES : (a + 1) * LANES] for a in range(count // LANES)]
    return jnp.concatenate(rows, axis=0).astype(BF16)


def is_low_core():
    return lax.axis_index("tm") % 2 == 0


def fill_strip(side, raw_ref, strip_ref):
    count = raw_ref.shape[0]
    strip_ref[0:count, :] = raw_ref[:, pl.ds(pl.multiple_of(side * (3 * LANES), LANES), LANES)]
    beside = raw_ref[:, pl.ds(pl.multiple_of(LANES + side * LANES, LANES), LANES)]
    strip_ref[count:, :] = beside_rows(beside, side * (LANES - 1))


def first_kernel(
    raw_ref, taps_ref, strip_ref, inner_taps_ref, far_taps_ref, near_taps_ref, beside, taps, sems
):
    side = lax.axis_index("tm") % 2
    count = raw_ref.shape[0]
    at = pl.multiple_of(side * (3 * LANES), LANES)
    by = pl.multiple_of(LANES + side * LANES, LANES)
    jobs = [
        pltpu.make_async_copy(raw_ref.at[:, pl.ds(by, LANES)], beside, sems.at[0]),
        pltpu.make_async_copy(raw_ref.at[:, pl.ds(at, LANES)], strip_ref.at[0:count], sems.at[1]),
    ]
    for job in jobs:
        job.start()

    @pl.when(side == 1)
    def _():
        job = pltpu.make_async_copy(taps_ref, taps, sems.at[2])
        job.start()
        job.wait()
        build_taps(False, taps, inner_taps_ref, far_taps_ref, near_taps_ref)

    jobs[0].wait()
    strip_ref[count:, :] = beside_rows(beside[...], side * (LANES - 1))
    jobs[1].wait()


def near_pack_kernel(
    raw_ref, after_ref, taps_ref, early_inner_ref, early_far_ref, early_near_ref,
    strip_ref, inner_taps_ref, far_taps_ref, near_taps_ref,
):
    del after_ref
    fill_strip(1 - lax.axis_index("tm") % 2, raw_ref, strip_ref)

    @pl.when(is_low_core())
    def _():
        build_taps(True, taps_ref, inner_taps_ref, far_taps_ref, near_taps_ref)

    @pl.when(jnp.logical_not(is_low_core()))
    def _():
        inner_taps_ref[...] = early_inner_ref[...]
        far_taps_ref[...] = early_far_ref[...]
        near_taps_ref[...] = early_near_ref[...]


def first(raw, taps):
    count, depth = raw.shape
    outs = [jax.ShapeDtypeStruct((count + 16, LANES), BF16)] + tap_shapes(taps, depth)
    return pl.pallas_call(
        first_kernel,
        in_specs=[pl.BlockSpec(memory_space=pltpu.HBM)] * 2,
        out_specs=[pl.BlockSpec(memory_space=pltpu.VMEM)] * len(outs),
        out_shape=outs,
        scratch_shapes=[
            pltpu.VMEM((count, LANES), BF16),
            pltpu.VMEM(taps.shape, F32),
            pltpu.SemaphoreType.DMA((3,)),
        ],
        compiler_params=pltpu.CompilerParams(vmem_limit_bytes=16 << 20),
        name="far_strip",
    )(*[pltpu.with_memory_space_constraint(a, pltpu.HBM) for a in (raw, taps)])


def near_pack(raw, after, taps, early):
    count, depth = raw.shape
    vmem = pl.BlockSpec(memory_space=pltpu.VMEM)
    return pl.pallas_call(
        near_pack_kernel,
        in_specs=[vmem, pl.BlockSpec(memory_space=pl.ANY)] + [vmem] * 4,
        out_specs=[vmem] * 4,
        out_shape=[jax.ShapeDtypeStruct((count + 16, LANES), BF16)] + tap_shapes(taps, depth),
        compiler_params=pltpu.CompilerParams(vmem_limit_bytes=8 << 20),
        cost_estimate=pl.CostEstimate(
            flops=2 * count * depth * 768, bytes_accessed=4 << 20, transcendentals=0
        ),
        name="near_strip",
    )(raw, after, taps, *early)


def combined(taps, columns, size, gains_ref, part):
    bands = lax.dot_general(taps, columns, NT, preferred_element_type=F32)
    held = gains_ref[0:1, part] * bands[0:size]
    for b in (1, 2):
        held = held + gains_ref[b : b + 1, part] * bands[b * size : (b + 1) * size]
    return held


def window_sums(columns_of, taps_ref, size, gains_ref, edges_of, onehot_ref, count, step, own_ref=None):
    sub = lax.broadcasted_iota(jnp.int32, (8, step), 0)
    total = None
    for start in range(0, count, step):
        part = slice(start, start + step)
        columns = columns_of(part)
        held = combined(taps_ref[:, 0 : columns.shape[1]], columns, size, gains_ref, part)
        if own_ref is not None:
            held = held + own_ref[:, part]
        first, last = held[0:8], held[size - 8 : size]
        if edges_of is not None:
            low, high = edges_of(start)
            first = first + jnp.where(sub == 0, low, 0.0)
            last = last + jnp.where(sub == 7, high, 0.0)
        middle = held[8 : size - 8]
        ahead = jnp.concatenate([middle, last, pltpu.roll(first, 7, 0)], axis=0)
        behind = jnp.concatenate([pltpu.roll(last, 1, 0), first, middle], axis=0)
        rate = (ahead - behind).astype(BF16)
        power = rate * jnp.abs(rate)
        term = lax.dot_general(onehot_ref[:, part], power, NT, preferred_element_type=F32)
        total = term if total is None else total + term
    return total


def sample_of_row(rows, size, cols):
    row = lax.broadcasted_iota(jnp.int32, (rows, cols), 0)
    return jnp.bitwise_and(row, 7) * (size // 8) + jnp.right_shift(row, 3)


def build_taps(is_low, taps_ref, inner_taps_ref, far_taps_ref, near_taps_ref):
    tm_pos = lax.axis_index("tm")
    inside = jnp.logical_and(tm_pos > 0, tm_pos < lax.axis_size("tm") - 1).astype(F32)
    depth = inner_taps_ref.shape[1]
    bands, width = taps_ref.shape
    wide = depth + LANES

    reach = 3 * LANES
    lane = lax.broadcasted_iota(jnp.int32, (bands, reach - 2 * LANES), 1)
    tail = jnp.where(lane == 0, taps_ref[:, width - 1 : width], 0.0)
    taps = jnp.concatenate([taps_ref[:, 0 : width - 1], tail], axis=1).astype(BF16)
    turn = (
        lax.broadcasted_iota(jnp.int32, (reach, wide), 0) + lax.broadcasted_iota(jnp.int32, (reach, wide), 1)
        == width - 1
    )
    base = jnp.dot(taps, turn.astype(F32).astype(BF16), preferred_element_type=F32)
    sub = lax.broadcasted_iota(jnp.int32, (8, depth), 0)

    row = lax.broadcasted_iota(jnp.int32, (8, wide), 0)

    def rows_of(b, size, shifts):
        line = jnp.broadcast_to(base[b : b + 1, :], (8, wide))
        spread = size // 8
        fan = line
        for i in range(1, 8):
            fan = jnp.where(row == i, pltpu.roll(line, i * spread, 1), fan)
        return [
            [pltpu.roll(fan, (j + shift) % wide, 1)[:, 0:depth] for j in range(spread)]
            for shift in shifts
        ]

    for b in range(bands):
        (rows,) = rows_of(b, INNER, (0,))
        for j in range(0, INNER // 8, 2):
            at = b * INNER + 8 * j
            inner_taps_ref[at : at + 16, :] = jnp.concatenate(rows[j : j + 2], axis=0).astype(BF16)
        low, high = rows_of(b, SIDE, (-1, 2 * LANES + 1 - SIDE))
        if is_low:
            low[0] = jnp.where(sub == 0, low[0] * inside, low[0])
        else:
            high[-1] = jnp.where(sub == 7, high[-1] * inside, high[-1])
        for j in range(0, SIDE // 8, 2):
            at = slice(b * SIDE + 8 * j, b * SIDE + 8 * j + 16)
            low_rows = jnp.concatenate(low[j : j + 2], axis=0).astype(BF16)
            high_rows = jnp.concatenate(high[j : j + 2], axis=0).astype(BF16)
            high_rows = jnp.concatenate([high_rows[:, 3 * LANES :], high_rows[:, : 3 * LANES]], axis=1)

            far_taps_ref[at, :], near_taps_ref[at, :] = (
                (low_rows, high_rows) if is_low else (high_rows, low_rows)
            )


def tap_shapes(taps, depth):
    rows = (INNER, SIDE, SIDE)
    return [jax.ShapeDtypeStruct((taps.shape[0] * r, depth), BF16) for r in rows]


def inner_kernel(
    levels_ref, length_ref, raw_ref, inner_taps_ref, taps_ref, index_ref, owner_ref, seat_ref,
    sums_ref, gains_ref, onehot_ref, divisor_ref,
):
    is_low = is_low_core()
    bands, width = taps_ref.shape
    blocks = index_ref.shape[1] // LANES
    index = index_ref[...]
    gains = jnp.zeros(index.shape, F32)
    for level in range(levels_ref.shape[1]):
        gains = jnp.where(index == level, levels_ref[:, level : level + 1], gains)
    gains = 0.5 * gains
    first = taps_ref[:, 0:1].astype(BF16).astype(F32)
    final = taps_ref[:, width - 1 : width].astype(BF16).astype(F32)
    low_edge = jnp.sum(gains * final, axis=0, keepdims=True)
    high_edge = jnp.sum(gains * first, axis=0, keepdims=True)
    gains_ref[0:bands, :] = gains
    gains_ref[3:4, :] = jnp.where(is_low, low_edge, high_edge)
    gains_ref[4:5, :] = jnp.where(is_low, high_edge, low_edge)
    mine = pl.ds(pl.multiple_of(lax.axis_index("chan") * blocks, blocks), blocks)
    place = seat_ref[mine, :] * lax.axis_size("chan") + owner_ref[mine, :]
    cable = lax.broadcasted_iota(jnp.int32, (onehot_ref.shape[0], LANES), 0)
    for a in range(blocks):
        onehot_ref[:, a * LANES : (a + 1) * LANES] = (cable == place[a : a + 1, :]).astype(F32).astype(BF16)
    tiles = divisor_ref.shape[0] // length_ref.shape[1]
    divisor_ref[...] = jnp.ones_like(divisor_ref)
    for k in range(length_ref.shape[1]):
        divisor_ref[k * tiles : (k + 1) * tiles, :] = jnp.broadcast_to(
            length_ref[:, k : k + 1].astype(F32), (tiles, LANES)
        )
    count = raw_ref.shape[0]
    sums_ref[...] = window_sums(
        lambda part: raw_ref[part, :], inner_taps_ref, INNER, gains_ref, None, onehot_ref, count, INNER_COLS
    )


def side_sums(is_low, edge_row, raw_ref, strip_ref, taps_ref, gains_ref, onehot_ref, own_ref=None):
    count = strip_ref.shape[0] - 16
    offset = pl.multiple_of(jnp.where(is_low, 0, LANES), LANES)
    beside = strip_ref[count:, :].astype(F32)

    def columns_of(part):
        if own_ref is not None:
            return strip_ref[part, :]
        return jnp.concatenate([strip_ref[part, :], raw_ref[part, pl.ds(offset, 3 * LANES)]], axis=1)

    def edges_of(start):
        rows = range(start // LANES, (start + SIDE_COLS) // LANES)
        line = jnp.concatenate([beside[a : a + 1, :] for a in rows], axis=1)
        line = line * gains_ref[edge_row : edge_row + 1, start : start + SIDE_COLS]
        return jnp.where(is_low, line, 0.0), jnp.where(is_low, 0.0, line)

    sums = window_sums(
        columns_of, taps_ref, SIDE, gains_ref, edges_of, onehot_ref, count, SIDE_COLS, own_ref
    )
    depth = taps_ref.shape[1]
    sample = sample_of_row(SIDE, SIDE, depth)
    sample = sample + jnp.where(is_low, -1, depth + 1 - SIDE)
    kept = (sample >= jnp.where(is_low, 0, depth - 1 - LANES)) & (
        sample <= jnp.where(is_low, LANES, depth - 1)
    )
    col = lax.broadcasted_iota(jnp.int32, (SIDE, depth), 1)
    order = ((col == sample) & kept).astype(F32).astype(BF16)
    return jnp.dot(sums.astype(BF16), order, preferred_element_type=F32)


def near_kernel(
    raw_ref, strip_ref, taps_ref, gains_ref, onehot_ref, inner_ref, far_taps_ref, sums_ref, own_ref
):
    count = raw_ref.shape[0]
    offset = pl.multiple_of(jnp.where(is_low_core(), 0, LANES), LANES)
    for start in range(0, count, SIDE_COLS):
        part = slice(start, start + SIDE_COLS)
        columns = raw_ref[part, pl.ds(offset, 3 * LANES)]
        own_ref[:, part] = combined(far_taps_ref[:, LANES:], columns, SIDE, gains_ref, part)
    near = side_sums(jnp.logical_not(is_low_core()), 4, raw_ref, strip_ref, taps_ref, gains_ref, onehot_ref)
    depth = raw_ref.shape[1]
    sample = sample_of_row(INNER, INNER, depth) + LANES
    kept = (sample > LANES) & (sample < depth - LANES - 1)
    col = lax.broadcasted_iota(jnp.int32, (INNER, depth), 1)
    order = ((col == sample) & kept).astype(F32).astype(BF16)
    sums_ref[...] = near + jnp.dot(inner_ref[...].astype(BF16), order, preferred_element_type=F32)


def far_kernel(strip_ref, taps_ref, gains_ref, onehot_ref, others_ref, own_ref, out_ref, scr):
    owners, pitch, _ = out_ref.shape
    seats = others_ref.shape[0] // owners
    far = side_sums(is_low_core(), 3, None, strip_ref, taps_ref, gains_ref, onehot_ref, own_ref)
    sums = others_ref[...] + far
    tiles = sums.shape[1] // LANES
    for spare in range(tiles * seats, pitch):
        scr[pl.ds(spare, owners, stride=pitch), :] = jnp.zeros((owners, LANES), F32)
    for s in range(seats):
        for j in range(tiles):
            scr[pl.ds(tiles * s + j, owners, stride=pitch), :] = sums[
                s * owners : (s + 1) * owners, j * LANES : (j + 1) * LANES
            ]
    for o in range(owners):
        out_ref[o, :, :] = scr[o * pitch : (o + 1) * pitch, :].astype(BF16)


def window(kernel, name, out_shape, scratch, flops, args):
    vmem = pl.BlockSpec(memory_space=pltpu.VMEM)
    many = isinstance(out_shape, list)
    return pl.pallas_call(
        kernel,
        in_specs=[vmem] * len(args),
        out_specs=[vmem] * len(out_shape) if many else vmem,
        out_shape=out_shape,
        scratch_shapes=scratch,
        compiler_params=pltpu.CompilerParams(vmem_limit_bytes=24 << 20),
        cost_estimate=pl.CostEstimate(flops=flops, bytes_accessed=4 << 20, transcendentals=0),
        name=name,
    )(*args)


def finish_kernel(divisor_ref, parts_ref, out_ref):
    seats, depth = out_ref.shape
    tiles = depth // LANES
    total = jnp.sum(parts_ref[...].astype(F32), axis=0) / divisor_ref[...]
    for s in range(seats):
        for j in range(tiles):
            row = tiles * s + j
            out_ref[s : s + 1, j * LANES : (j + 1) * LANES] = total[row : row + 1]


def finish(parts, divisor, seats, depth):
    vmem = pl.BlockSpec(memory_space=pltpu.VMEM)
    return pl.pallas_call(
        finish_kernel,
        in_specs=[vmem, vmem],
        out_specs=vmem,
        out_shape=jax.ShapeDtypeStruct((seats, depth), F32),
        compiler_params=pltpu.CompilerParams(vmem_limit_bytes=4 << 20),
        name="finish_sum",
    )(divisor, parts)


def shards(raw, band_taps, band_gain, gain_index, owner_of, seat, cable_length):
    tm_count = lax.axis_size("tm")
    chan_count = lax.axis_size("chan")
    depth = raw.shape[1]
    far_pairs = [(i, i + 1) for i in range(1, tm_count - 1, 2)]
    far_pairs = far_pairs + [(j, i) for i, j in far_pairs]
    near_pairs = [(i, i ^ 1) for i in range(tm_count)]
    cab_dev = cable_length.shape[0]
    cables = cab_dev * chan_count

    far_sent, *early = first(raw, band_taps)
    far_strip = lax.ppermute(far_sent, "tm", far_pairs)
    near_sent, inner_taps, far_taps, near_taps = near_pack(raw, far_sent, band_taps, early)
    near_strip = lax.ppermute(near_sent, "tm", near_pairs)
    pitch = -(-(depth // LANES) * cab_dev // 8) * 8
    work = 2 * raw.shape[0] * depth * inner_taps.shape[0]
    inner_sums, gains, onehot, divisor = window(
        inner_kernel, "inner_window",
        [
            jax.ShapeDtypeStruct((cables, INNER), F32),
            jax.ShapeDtypeStruct((8, raw.shape[0]), F32),
            jax.ShapeDtypeStruct((cables, raw.shape[0]), BF16),
            jax.ShapeDtypeStruct((pitch, LANES), F32),
        ],
        [], 50 * work,
        (
            band_gain.reshape(1, -1), cable_length.reshape(1, -1), raw, inner_taps, band_taps,
            gain_index.T, owner_of.reshape(-1, LANES), seat.reshape(-1, LANES),
        ),
    )
    others, own = window(
        near_kernel, "near_window",
        [jax.ShapeDtypeStruct((cables, depth), F32), jax.ShapeDtypeStruct((SIDE, raw.shape[0]), F32)],
        [], work, (raw, near_strip, near_taps, gains, onehot, inner_sums, far_taps),
    )
    parts = window(
        far_kernel, "far_window", jax.ShapeDtypeStruct((chan_count, pitch, LANES), BF16),
        [pltpu.VMEM((chan_count * pitch, LANES), F32)], work,
        (far_strip, far_taps, gains, onehot, others, own),
    )
    parts = lax.all_to_all(parts, "chan", split_axis=0, concat_axis=0, tiled=True)
    return finish(parts, divisor, cab_dev, depth)


def solution(mesh):
    return jax.shard_map(
        shards,
        mesh=mesh,
        in_specs=(P("chan", "tm"), P(), P(), P("chan", None), P(), P(), P("chan")),
        out_specs=P("chan", "tm"),
        check_vma=False,
    )
```

```python
import jax
import jax.numpy as jnp
from jax import lax
from jax.experimental import pallas as pl
from jax.experimental.pallas import tpu as pltpu
from jax.sharding import PartitionSpec as P

LANES = 128
SIDE = 144
INNER = 256
SIDE_COLS = 2048
INNER_COLS = 2048
F32 = jnp.float32
BF16 = jnp.bfloat16
NT = (((1,), (1,)), ((), ()))


def beside_rows(beside, lane_at):
    count = beside.shape[0]
    lane = lax.broadcasted_iota(jnp.int32, (16, LANES), 1)
    pick = (lane == lane_at).astype(F32).astype(BF16)
    column = lax.dot_general(pick, beside, NT, preferred_element_type=F32)
    rows = [column[0:1, a * LANES : (a + 1) * LANES] for a in range(count // LANES)]
    return jnp.concatenate(rows, axis=0).astype(BF16)


def is_low_core():
    return lax.axis_index("tm") % 2 == 0


def fill_strip(side, raw_ref, strip_ref):
    count = raw_ref.shape[0]
    strip_ref[0:count, :] = raw_ref[:, pl.ds(pl.multiple_of(side * (3 * LANES), LANES), LANES)]
    beside = raw_ref[:, pl.ds(pl.multiple_of(LANES + side * LANES, LANES), LANES)]
    strip_ref[count:, :] = beside_rows(beside, side * (LANES - 1))


def first_kernel(
    raw_ref, taps_ref, strip_ref, inner_taps_ref, far_taps_ref, near_taps_ref, beside, taps, sems
):
    side = lax.axis_index("tm") % 2
    count = raw_ref.shape[0]
    at = pl.multiple_of(side * (3 * LANES), LANES)
    by = pl.multiple_of(LANES + side * LANES, LANES)
    jobs = [
        pltpu.make_async_copy(raw_ref.at[:, pl.ds(by, LANES)], beside, sems.at[0]),
        pltpu.make_async_copy(raw_ref.at[:, pl.ds(at, LANES)], strip_ref.at[0:count], sems.at[1]),
    ]
    for job in jobs:
        job.start()

    @pl.when(side == 1)
    def _():
        job = pltpu.make_async_copy(taps_ref, taps, sems.at[2])
        job.start()
        job.wait()
        build_taps(False, taps, inner_taps_ref, far_taps_ref, near_taps_ref)

    jobs[0].wait()
    strip_ref[count:, :] = beside_rows(beside[...], side * (LANES - 1))
    jobs[1].wait()


def near_pack_kernel(
    raw_ref, after_ref, taps_ref, early_inner_ref, early_far_ref, early_near_ref,
    strip_ref, inner_taps_ref, far_taps_ref, near_taps_ref,
):
    del after_ref
    fill_strip(1 - lax.axis_index("tm") % 2, raw_ref, strip_ref)

    @pl.when(is_low_core())
    def _():
        build_taps(True, taps_ref, inner_taps_ref, far_taps_ref, near_taps_ref)

    @pl.when(jnp.logical_not(is_low_core()))
    def _():
        inner_taps_ref[...] = early_inner_ref[...]
        far_taps_ref[...] = early_far_ref[...]
        near_taps_ref[...] = early_near_ref[...]


def first(raw, taps):
    count, depth = raw.shape
    outs = [jax.ShapeDtypeStruct((count + 16, LANES), BF16)] + tap_shapes(taps, depth)
    return pl.pallas_call(
        first_kernel,
        in_specs=[pl.BlockSpec(memory_space=pltpu.HBM)] * 2,
        out_specs=[pl.BlockSpec(memory_space=pltpu.VMEM)] * len(outs),
        out_shape=outs,
        scratch_shapes=[
            pltpu.VMEM((count, LANES), BF16),
            pltpu.VMEM(taps.shape, F32),
            pltpu.SemaphoreType.DMA((3,)),
        ],
        compiler_params=pltpu.CompilerParams(vmem_limit_bytes=16 << 20),
        name="far_strip",
    )(*[pltpu.with_memory_space_constraint(a, pltpu.HBM) for a in (raw, taps)])


def near_pack(raw, after, taps, early):
    count, depth = raw.shape
    vmem = pl.BlockSpec(memory_space=pltpu.VMEM)
    return pl.pallas_call(
        near_pack_kernel,
        in_specs=[vmem, pl.BlockSpec(memory_space=pl.ANY)] + [vmem] * 4,
        out_specs=[vmem] * 4,
        out_shape=[jax.ShapeDtypeStruct((count + 16, LANES), BF16)] + tap_shapes(taps, depth),
        compiler_params=pltpu.CompilerParams(vmem_limit_bytes=8 << 20),
        cost_estimate=pl.CostEstimate(
            flops=2 * count * depth * 768, bytes_accessed=4 << 20, transcendentals=0
        ),
        name="near_strip",
    )(raw, after, taps, *early)


def combined(taps, columns, size, gains_ref, part):
    bands = lax.dot_general(taps, columns, NT, preferred_element_type=F32)
    held = gains_ref[0:1, part] * bands[0:size]
    for b in (1, 2):
        held = held + gains_ref[b : b + 1, part] * bands[b * size : (b + 1) * size]
    return held


def window_sums(columns_of, taps_ref, size, gains_ref, edges_of, onehot_ref, count, step, own_ref=None):
    sub = lax.broadcasted_iota(jnp.int32, (8, step), 0)
    total = None
    for start in range(0, count, step):
        part = slice(start, start + step)
        columns = columns_of(part)
        held = combined(taps_ref[:, 0 : columns.shape[1]], columns, size, gains_ref, part)
        if own_ref is not None:
            held = held + own_ref[:, part]
        first, last = held[0:8], held[size - 8 : size]
        if edges_of is not None:
            low, high = edges_of(start)
            first = first + jnp.where(sub == 0, low, 0.0)
            last = last + jnp.where(sub == 7, high, 0.0)
        middle = held[8 : size - 8]
        ahead = jnp.concatenate([middle, last, pltpu.roll(first, 7, 0)], axis=0)
        behind = jnp.concatenate([pltpu.roll(last, 1, 0), first, middle], axis=0)
        rate = (ahead - behind).astype(BF16)
        power = rate * jnp.abs(rate)
        term = lax.dot_general(onehot_ref[:, part], power, NT, preferred_element_type=F32)
        total = term if total is None else total + term
    return total


def sample_of_row(rows, size, cols):
    row = lax.broadcasted_iota(jnp.int32, (rows, cols), 0)
    return jnp.bitwise_and(row, 7) * (size // 8) + jnp.right_shift(row, 3)


def build_taps(is_low, taps_ref, inner_taps_ref, far_taps_ref, near_taps_ref):
    tm_pos = lax.axis_index("tm")
    inside = jnp.logical_and(tm_pos > 0, tm_pos < lax.axis_size("tm") - 1).astype(F32)
    depth = inner_taps_ref.shape[1]
    bands, width = taps_ref.shape
    wide = depth + LANES

    reach = 3 * LANES
    lane = lax.broadcasted_iota(jnp.int32, (bands, reach - 2 * LANES), 1)
    tail = jnp.where(lane == 0, taps_ref[:, width - 1 : width], 0.0)
    taps = jnp.concatenate([taps_ref[:, 0 : width - 1], tail], axis=1).astype(BF16)
    turn = (
        lax.broadcasted_iota(jnp.int32, (reach, wide), 0) + lax.broadcasted_iota(jnp.int32, (reach, wide), 1)
        == width - 1
    )
    base = jnp.dot(taps, turn.astype(F32).astype(BF16), preferred_element_type=F32)
    sub = lax.broadcasted_iota(jnp.int32, (8, depth), 0)

    row = lax.broadcasted_iota(jnp.int32, (8, wide), 0)

    def rows_of(b, size, shifts):
        line = jnp.broadcast_to(base[b : b + 1, :], (8, wide))
        spread = size // 8
        fan = line
        for i in range(1, 8):
            fan = jnp.where(row == i, pltpu.roll(line, i * spread, 1), fan)
        return [
            [pltpu.roll(fan, (j + shift) % wide, 1)[:, 0:depth] for j in range(spread)]
            for shift in shifts
        ]

    for b in range(bands):
        (rows,) = rows_of(b, INNER, (0,))
        for j in range(0, INNER // 8, 2):
            at = b * INNER + 8 * j
            inner_taps_ref[at : at + 16, :] = jnp.concatenate(rows[j : j + 2], axis=0).astype(BF16)
        low, high = rows_of(b, SIDE, (-1, 2 * LANES + 1 - SIDE))
        if is_low:
            low[0] = jnp.where(sub == 0, low[0] * inside, low[0])
        else:
            high[-1] = jnp.where(sub == 7, high[-1] * inside, high[-1])
        for j in range(0, SIDE // 8, 2):
            at = slice(b * SIDE + 8 * j, b * SIDE + 8 * j + 16)
            low_rows = jnp.concatenate(low[j : j + 2], axis=0).astype(BF16)
            high_rows = jnp.concatenate(high[j : j + 2], axis=0).astype(BF16)
            high_rows = jnp.concatenate([high_rows[:, 3 * LANES :], high_rows[:, : 3 * LANES]], axis=1)

            far_taps_ref[at, :], near_taps_ref[at, :] = (
                (low_rows, high_rows) if is_low else (high_rows, low_rows)
            )


def tap_shapes(taps, depth):
    rows = (INNER, SIDE, SIDE)
    return [jax.ShapeDtypeStruct((taps.shape[0] * r, depth), BF16) for r in rows]


def inner_kernel(
    levels_ref, length_ref, raw_ref, inner_taps_ref, taps_ref, index_ref, owner_ref, seat_ref,
    sums_ref, gains_ref, onehot_ref, divisor_ref,
):
    is_low = is_low_core()
    bands, width = taps_ref.shape
    blocks = index_ref.shape[1] // LANES
    index = index_ref[...]
    gains = jnp.zeros(index.shape, F32)
    for level in range(levels_ref.shape[1]):
        gains = jnp.where(index == level, levels_ref[:, level : level + 1], gains)
    gains = 0.5 * gains
    first = taps_ref[:, 0:1].astype(BF16).astype(F32)
    final = taps_ref[:, width - 1 : width].astype(BF16).astype(F32)
    low_edge = jnp.sum(gains * final, axis=0, keepdims=True)
    high_edge = jnp.sum(gains * first, axis=0, keepdims=True)
    gains_ref[0:bands, :] = gains
    gains_ref[3:4, :] = jnp.where(is_low, low_edge, high_edge)
    gains_ref[4:5, :] = jnp.where(is_low, high_edge, low_edge)
    mine = pl.ds(pl.multiple_of(lax.axis_index("chan") * blocks, blocks), blocks)
    place = seat_ref[mine, :] * lax.axis_size("chan") + owner_ref[mine, :]
    cable = lax.broadcasted_iota(jnp.int32, (onehot_ref.shape[0], LANES), 0)
    for a in range(blocks):
        onehot_ref[:, a * LANES : (a + 1) * LANES] = (cable == place[a : a + 1, :]).astype(F32).astype(BF16)
    tiles = divisor_ref.shape[0] // length_ref.shape[1]
    divisor_ref[...] = jnp.ones_like(divisor_ref)
    for k in range(length_ref.shape[1]):
        divisor_ref[k * tiles : (k + 1) * tiles, :] = jnp.broadcast_to(
            length_ref[:, k : k + 1].astype(F32), (tiles, LANES)
        )
    count = raw_ref.shape[0]
    sums_ref[...] = window_sums(
        lambda part: raw_ref[part, :], inner_taps_ref, INNER, gains_ref, None, onehot_ref, count, INNER_COLS
    )


def side_sums(is_low, edge_row, raw_ref, strip_ref, taps_ref, gains_ref, onehot_ref, own_ref=None):
    count = strip_ref.shape[0] - 16
    offset = pl.multiple_of(jnp.where(is_low, 0, LANES), LANES)
    beside = strip_ref[count:, :].astype(F32)

    def columns_of(part):
        if own_ref is not None:
            return strip_ref[part, :]
        return jnp.concatenate([strip_ref[part, :], raw_ref[part, pl.ds(offset, 3 * LANES)]], axis=1)

    def edges_of(start):
        rows = range(start // LANES, (start + SIDE_COLS) // LANES)
        line = jnp.concatenate([beside[a : a + 1, :] for a in rows], axis=1)
        line = line * gains_ref[edge_row : edge_row + 1, start : start + SIDE_COLS]
        return jnp.where(is_low, line, 0.0), jnp.where(is_low, 0.0, line)

    sums = window_sums(
        columns_of, taps_ref, SIDE, gains_ref, edges_of, onehot_ref, count, SIDE_COLS, own_ref
    )
    depth = taps_ref.shape[1]
    sample = sample_of_row(SIDE, SIDE, depth)
    sample = sample + jnp.where(is_low, -1, depth + 1 - SIDE)
    kept = (sample >= jnp.where(is_low, 0, depth - 1 - LANES)) & (
        sample <= jnp.where(is_low, LANES, depth - 1)
    )
    col = lax.broadcasted_iota(jnp.int32, (SIDE, depth), 1)
    order = ((col == sample) & kept).astype(F32).astype(BF16)
    return jnp.dot(sums.astype(BF16), order, preferred_element_type=F32)


def near_kernel(
    raw_ref, strip_ref, taps_ref, gains_ref, onehot_ref, inner_ref, far_taps_ref, sums_ref, own_ref
):
    count = raw_ref.shape[0]
    offset = pl.multiple_of(jnp.where(is_low_core(), 0, LANES), LANES)
    for start in range(0, count, SIDE_COLS):
        part = slice(start, start + SIDE_COLS)
        columns = raw_ref[part, pl.ds(offset, 3 * LANES)]
        own_ref[:, part] = combined(far_taps_ref[:, LANES:], columns, SIDE, gains_ref, part)
    near = side_sums(jnp.logical_not(is_low_core()), 4, raw_ref, strip_ref, taps_ref, gains_ref, onehot_ref)
    depth = raw_ref.shape[1]
    sample = sample_of_row(INNER, INNER, depth) + LANES
    kept = (sample > LANES) & (sample < depth - LANES - 1)
    col = lax.broadcasted_iota(jnp.int32, (INNER, depth), 1)
    order = ((col == sample) & kept).astype(F32).astype(BF16)
    sums_ref[...] = near + jnp.dot(inner_ref[...].astype(BF16), order, preferred_element_type=F32)


def far_kernel(strip_ref, taps_ref, gains_ref, onehot_ref, others_ref, own_ref, out_ref, scr):
    owners, pitch, _ = out_ref.shape
    seats = others_ref.shape[0] // owners
    far = side_sums(is_low_core(), 3, None, strip_ref, taps_ref, gains_ref, onehot_ref, own_ref)
    sums = others_ref[...] + far
    tiles = sums.shape[1] // LANES
    for spare in range(tiles * seats, pitch):
        scr[pl.ds(spare, owners, stride=pitch), :] = jnp.zeros((owners, LANES), F32)
    for s in range(seats):
        for j in range(tiles):
            scr[pl.ds(tiles * s + j, owners, stride=pitch), :] = sums[
                s * owners : (s + 1) * owners, j * LANES : (j + 1) * LANES
            ]
    for o in range(owners):
        out_ref[o, :, :] = scr[o * pitch : (o + 1) * pitch, :].astype(BF16)


def window(kernel, name, out_shape, scratch, flops, args):
    vmem = pl.BlockSpec(memory_space=pltpu.VMEM)
    many = isinstance(out_shape, list)
    return pl.pallas_call(
        kernel,
        in_specs=[vmem] * len(args),
        out_specs=[vmem] * len(out_shape) if many else vmem,
        out_shape=out_shape,
        scratch_shapes=scratch,
        compiler_params=pltpu.CompilerParams(vmem_limit_bytes=24 << 20),
        cost_estimate=pl.CostEstimate(flops=flops, bytes_accessed=4 << 20, transcendentals=0),
        name=name,
    )(*args)


def finish_kernel(divisor_ref, parts_ref, out_ref):
    seats, depth = out_ref.shape
    tiles = depth // LANES
    total = jnp.sum(parts_ref[...].astype(F32), axis=0) / divisor_ref[...]
    for s in range(seats):
        for j in range(tiles):
            row = tiles * s + j
            out_ref[s : s + 1, j * LANES : (j + 1) * LANES] = total[row : row + 1]


def finish(parts, divisor, seats, depth):
    vmem = pl.BlockSpec(memory_space=pltpu.VMEM)
    return pl.pallas_call(
        finish_kernel,
        in_specs=[vmem, vmem],
        out_specs=vmem,
        out_shape=jax.ShapeDtypeStruct((seats, depth), F32),
        compiler_params=pltpu.CompilerParams(vmem_limit_bytes=4 << 20),
        name="finish_sum",
    )(divisor, parts)


def shards(raw, band_taps, band_gain, gain_index, owner_of, seat, cable_length):
    tm_count = lax.axis_size("tm")
    chan_count = lax.axis_size("chan")
    depth = raw.shape[1]
    far_pairs = [(i, i + 1) for i in range(1, tm_count - 1, 2)]
    far_pairs = far_pairs + [(j, i) for i, j in far_pairs]
    near_pairs = [(i, i ^ 1) for i in range(tm_count)]
    cab_dev = cable_length.shape[0]
    cables = cab_dev * chan_count

    far_sent, *early = first(raw, band_taps)
    far_strip = lax.ppermute(far_sent, "tm", far_pairs)
    near_sent, inner_taps, far_taps, near_taps = near_pack(raw, far_sent, band_taps, early)
    near_strip = lax.ppermute(near_sent, "tm", near_pairs)
    pitch = -(-(depth // LANES) * cab_dev // 8) * 8
    work = 2 * raw.shape[0] * depth * inner_taps.shape[0]
    inner_sums, gains, onehot, divisor = window(
        inner_kernel, "inner_window",
        [
            jax.ShapeDtypeStruct((cables, INNER), F32),
            jax.ShapeDtypeStruct((8, raw.shape[0]), F32),
            jax.ShapeDtypeStruct((cables, raw.shape[0]), BF16),
            jax.ShapeDtypeStruct((pitch, LANES), F32),
        ],
        [], 50 * work,
        (
            band_gain.reshape(1, -1), cable_length.reshape(1, -1), raw, inner_taps, band_taps,
            gain_index.T, owner_of.reshape(-1, LANES), seat.reshape(-1, LANES),
        ),
    )
    others, own = window(
        near_kernel, "near_window",
        [jax.ShapeDtypeStruct((cables, depth), F32), jax.ShapeDtypeStruct((SIDE, raw.shape[0]), F32)],
        [], work, (raw, near_strip, near_taps, gains, onehot, inner_sums, far_taps),
    )
    parts = window(
        far_kernel, "far_window", jax.ShapeDtypeStruct((chan_count, pitch, LANES), BF16),
        [pltpu.VMEM(((chan_count + 1) * pitch, LANES), F32)], work,
        (far_strip, far_taps, gains, onehot, others, own),
    )
    parts = lax.all_to_all(parts, "chan", split_axis=0, concat_axis=0, tiled=True)
    return finish(parts, divisor, cab_dev, depth)


def solution(mesh):
    return jax.shard_map(
        shards,
        mesh=mesh,
        in_specs=(P("chan", "tm"), P(), P(), P("chan", None), P(), P(), P("chan")),
        out_specs=P("chan", "tm"),
        check_vma=False,
    )
```
